128 devices in a mesh: freq: 4 (over z), chan: 32 (over x, y, core).
Axes of the slice: x: 4, y: 4, z: 4, core: 2. Of those that a mesh axis runs over, the one named last changes fastest.
Arguments:
- raw_strain: bfloat16 [32, 32, 150000], P('chan', 'freq'), may hold values from -6 to 6
- fir_taps: bfloat16 [20], replicated, may hold values from -1.25 to 1.25
- band_bins: int32 [240], replicated, may hold values from 60 to 359, as said below
- live_mask: int32 [32, 32], P('chan', 'freq'), may hold values 0 or 1
Outputs:
- cross_spectra: float32 [240, 2, 1024, 1024], P('freq', None, 'chan')
The draws below stay inside these ranges and needn't reach their ends.
Inputs may be any that keep to these rules, and one draw needn't show every extreme that they name: `band_bins`: strictly increasing; the first is 60 and the last is 359.
All inputs are finite; a program needn't handle non-finite values. No bound on the sum of `live_mask` on one device may be relied on, other than what follows from the above.
Results may differ from the reference program's by a relative error of at most 0.0067.
Values may be sent and summed in bfloat16 or wider, within the bound.
A program may use at most 64 MiB of HBM per device.

```python
import math
import jax
import jax.numpy as jnp
from jax import lax

CH_DEV = 32
C = 1024
WIN = 10
DECIM = 10
TAPS = 20
NT = 1500
FB = 240
SPAN = 300
LOW = 60
N_CHAN = 32


def draw_band_bins(key, part):
    inner = SPAN - 2
    scores = jax.random.randint(key, (inner,), 0, 1000, dtype=jnp.int32) * inner + jnp.arange(inner, dtype=jnp.int32)
    values, picked = lax.top_k(scores, FB - 2)
    chosen = jnp.sort(picked.astype(jnp.int32)) + LOW + 1
    first = jnp.full((1,), LOW, dtype=jnp.int32)
    last = jnp.full((1,), LOW + SPAN - 1, dtype=jnp.int32)
    return jnp.concatenate([first, chosen, last]).astype(jnp.int32)


def set_ends(entries, own_key, low, largest):
    spot = [jax.random.randint(jax.random.fold_in(own_key, axis), (), 0, length) for axis, length in enumerate(entries.shape)]
    main_axis = entries.shape.index(max(entries.shape))
    beside = spot[:main_axis] + [(spot[main_axis] + 1) % entries.shape[main_axis]] + spot[main_axis + 1:]
    return entries.at[tuple(spot)].set(low).at[tuple(beside)].set(largest)


def block_scale(stream_key, extent, pieces, smallest, high):
    def one(axis_at, parts):
        heights = jax.random.uniform(jax.random.fold_in(jax.random.fold_in(stream_key, 6), axis_at), (parts,), jnp.float32, smallest / len(pieces), high / len(pieces))
        return jnp.repeat(jnp.exp(heights), extent[axis_at] // parts).reshape((-1,) + (1,) * (len(extent) - axis_at - 1))

    loudness = one(*pieces[0])
    for cut in pieces[1:]:
        loudness = loudness * one(*cut)
    return loudness


def gaussian(stream_key, shape, spread, limit, shards=(), held_as=jnp.bfloat16):
    array = spread * jax.random.normal(stream_key, shape, jnp.float32)
    if shards:
        array = array * block_scale(stream_key, shape, shards, -0.22, 0.18)
    return jnp.clip(array, -limit, limit).astype(held_as)


def setup_inputs(seed: int = 0) -> dict:
    streams_of = jax.random.split(jax.random.key(seed), 5)
    raw_strain = gaussian(streams_of[0], (N_CHAN, CH_DEV, WIN * NT * DECIM), 1.0, 6.0, ((0, 32), (1, 4)))
    fir_taps = gaussian(streams_of[1], (TAPS,), TAPS ** -0.5, 1.25)
    band_bins = draw_band_bins(jax.random.fold_in(streams_of[4], 71), 0)
    live_mask = set_ends((jax.random.randint(streams_of[3], (N_CHAN, CH_DEV), 0, 10) < 9).astype(jnp.int32), jax.random.fold_in(streams_of[3], 1), 0, 1)
    return dict(raw_strain=raw_strain, fir_taps=fir_taps, band_bins=band_bins, live_mask=live_mask)


def make_table(band_bins):
    times = jnp.arange(NT, dtype=jnp.int32)[:, None]
    phase = times * band_bins[None, :].astype(jnp.int32) % NT
    angle = phase.astype(jnp.float32) * jnp.float32(2.0 * math.pi / NT)
    return jnp.concatenate([jnp.cos(angle), -jnp.sin(angle)], axis=1).astype(jnp.bfloat16)

def prepare(block, fir_taps, table, mask_row):
    rows = block.shape[0]
    samples = block.reshape(rows * WIN * NT, DECIM)
    tap_cols = jnp.transpose(fir_taps.reshape(2, DECIM)[:, ::-1])
    part = jnp.dot(samples, tap_cols, preferred_element_type=jnp.float32).reshape(rows, WIN, NT, 2)
    previous = jnp.pad(part[..., 1], ((0, 0), (0, 0), (1, 0)))[..., :NT]
    decimated = (part[..., 0] + previous).astype(jnp.bfloat16)
    spectrum = jnp.dot(decimated.reshape(rows * WIN, NT), table, preferred_element_type=jnp.float32)
    spectrum = spectrum.reshape(rows, WIN, 2, FB)
    power = lax.optimization_barrier(jnp.sum(spectrum * spectrum, axis=(2, 3))) / FB
    scale = lax.rsqrt(power + 1e-06) * mask_row.astype(jnp.float32)[:, None]
    return (spectrum * scale[:, :, None, None]).astype(jnp.bfloat16)

def reference(raw_strain, fir_taps, band_bins, live_mask):
    table = make_table(band_bins)

    def one_block(pair):
        block, mask_row = pair
        return prepare(block, fir_taps, table, mask_row)
    whitened = lax.map(one_block, (raw_strain, live_mask))
    whitened = whitened.reshape(C, WIN, 2, FB)
    ordered = jnp.transpose(whitened, (3, 2, 1, 0))

    def one_bin(spec):
        spec32 = spec.astype(jnp.float32)
        prod = jnp.einsum('awi,bwj->abij', spec32, spec32)
        real_part = prod[0, 0] + prod[1, 1]
        imag_part = prod[1, 0] - prod[0, 1]
        return jnp.stack([real_part, imag_part], axis=0) / WIN
    return lax.map(one_bin, ordered)
```

```python
import functools
import math

import jax
import jax.numpy as jnp
from jax import lax
from jax.experimental import pallas as pl
from jax.experimental.pallas import tpu as pltpu
from jax.sharding import PartitionSpec as P

WIN = 10
DECIM = 10
NT = 1500
TAPS = 20
BINS = 240
ROWS = 8
TILE = 128
SPAN = TILE * DECIM
SAMPLES = WIN * NT * DECIM
TILES = -(-SAMPLES // SPAN)
NTP = 12 * TILE
GROUP = 12
PACK = 5 * TILE
WIDE = 5 * 256
F32 = jnp.float32
BF16 = jnp.bfloat16
I32 = jnp.int32
MESH = pl.DeviceIdType.MESH


def iota(shape, axis):
    return lax.broadcasted_iota(I32, shape, axis)


def build_fir(taps_ref, fir_ref):
    row = iota((80, TAPS), 0)
    phase = row % DECIM
    tap = iota((80, TAPS), 1)
    taps = jnp.broadcast_to(taps_ref[...].astype(F32), (80, TAPS))
    near = jnp.sum(jnp.where(tap == 9 - phase, taps, 0.0), axis=1, keepdims=True)
    far = jnp.sum(jnp.where(tap == 19 - phase, taps, 0.0), axis=1, keepdims=True)
    near = jnp.broadcast_to(near, (80, 256))
    far = jnp.broadcast_to(far, (80, 256))
    gap = iota((80, 256), 1) - iota((80, 256), 0) // DECIM
    for step in range(SPAN // 80):
        block = jnp.where(gap == 8 * step, near, jnp.where(gap == 8 * step + 1, far, 0.0))
        fir_ref[80 * step : 80 * step + 80, :] = block.astype(BF16)


def build_table(bins_ref, table_ref):
    bins = bins_ref[...].astype(F32)
    bins = jnp.concatenate([bins, jnp.zeros((1, 16), F32)], axis=1)
    row = iota((40, 256), 0)
    times = jnp.where(row < 8, row, jnp.where(row < 24, 8 * (row - 8), 128 * (row - 24)))
    product = times.astype(F32) * bins
    turns = jnp.floor(product * (1.0 / NT))
    left = product - turns * NT
    left = jnp.where(left < 0, left + NT, left)
    left = jnp.where(left >= NT, left - NT, left)
    angle = left * F32(2.0 * math.pi / NT)
    re = jnp.cos(angle)
    im = -jnp.sin(angle)
    kept = iota((40, 256), 1) < BINS
    re = jnp.where(kept, re, 0.0)
    im = jnp.where(kept, im, 0.0)
    base_re, base_im = [], []
    for b in range(16):
        tr, ti = re[8 + b : 9 + b], im[8 + b : 9 + b]
        base_re.append(re[0:8] * tr - im[0:8] * ti)
        base_im.append(re[0:8] * ti + im[0:8] * tr)
    base_re = jnp.concatenate(base_re, axis=0)
    base_im = jnp.concatenate(base_im, axis=0)
    for a in range(12):
        tr, ti = re[24 + a : 25 + a], im[24 + a : 25 + a]
        block_re = base_re * tr - base_im * ti
        block_im = base_re * ti + base_im * tr
        if a == 11:
            inside = iota((TILE, 256), 0) < NT - 11 * TILE
            block_re = jnp.where(inside, block_re, 0.0)
            block_im = jnp.where(inside, block_im, 0.0)
        table_ref[TILE * a : TILE * a + TILE, 0:256] = block_re.astype(BF16)
        table_ref[TILE * a : TILE * a + TILE, 256:512] = block_im.astype(BF16)


def build_left(x_ref, left_ref):
    def tile(t):
        return x_ref[0, :, SPAN * t : min(SPAN * t + SPAN, SAMPLES)].astype(F32)

    blocks = []
    for t in range(TILES):
        blocks.append((t, None))
    for w in range(1, WIN):
        t = NT * w // TILE
        blocks.append((t, NT * DECIM * w - SPAN * t))
    blocks.append((None, None))

    def value(block):
        t, first = block
        if t is None:
            return jnp.zeros((ROWS, SPAN), F32)
        part = tile(t)
        if part.shape[1] < SPAN:
            part = jnp.concatenate([part, jnp.zeros((ROWS, SPAN - part.shape[1]), F32)], axis=1)
        if first is not None:
            part = jnp.where(iota((ROWS, SPAN), 1) < first, 0.0, part)
        return part

    for pair in range(len(blocks) // 2):
        both = jnp.concatenate([value(blocks[2 * pair]), value(blocks[2 * pair + 1])], axis=0)
        left_ref[16 * pair : 16 * pair + 16, :] = both.astype(BF16)


def align_windows(res_ref, dec_ref):
    lane = iota((ROWS, TILE), 1)

    def plain(t):
        main = res_ref[8 * t : 8 * t + 8, 0:TILE]
        if t == 0:
            return main
        return main + res_ref[8 * t - 8 : 8 * t, TILE : 2 * TILE]

    def window(w):
        t = NT * w // TILE
        shift = NT * w - TILE * t
        tiles = [plain(t + u) for u in range(1, 13 if shift else 12)]
        if w == 0:
            first = plain(0)
        else:
            at = 8 * (TILES + w - 1)
            first = res_ref[at : at + 8, 0:TILE]
        tiles = [first] + tiles
        if shift:
            rolled = [pltpu.roll(one, TILE - shift, 1) for one in tiles]
            tiles = [
                jnp.where(lane < TILE - shift, rolled[u], rolled[u + 1]) for u in range(12)
            ]
        return jnp.concatenate(tiles, axis=1)

    for pair in range(WIN // 2):
        both = jnp.concatenate([window(2 * pair), window(2 * pair + 1)], axis=0)
        dec_ref[16 * pair : 16 * pair + 16, :] = both.astype(BF16)


def pack(white, send_ref):
    lane = iota((ROWS, 256), 1)
    segment = lane // GROUP
    wrapped = (lane + 256) // GROUP
    turned = []
    for part in range(2):
        for w in range(WIN):
            spot = part * WIN + w
            piece = white[8 * w : 8 * w + 8, 256 * part : 256 * part + 256]
            turned.append(pltpu.roll(piece, GROUP * spot, 1) if spot else piece)
    for group in range(BINS // GROUP):
        halves = []
        for half in range(2):
            lanes = slice(TILE * half, TILE * half + TILE)
            total = jnp.zeros((ROWS, TILE), F32)
            for spot in range(2 * WIN):
                start = GROUP * (spot + group)
                covers = [
                    at
                    for at in (start, start - 256)
                    if at < TILE * half + TILE and at + GROUP > TILE * half
                ]
                for at in covers:
                    ids = segment if at == start else wrapped
                    total = jnp.where(
                        ids[:, lanes] == spot + group, turned[spot][:, lanes], total
                    )
            halves.append(total)
        dest = jnp.concatenate(halves, axis=1)
        if group:
            dest = pltpu.roll(dest, 256 - GROUP * group, 1)
        both = jnp.concatenate([dest[:, 0:TILE], dest[:, TILE:256]], axis=0)
        z, g = group // 5, group % 5
        send_ref[z, :, TILE * g : TILE * g + TILE] = both.astype(BF16)


def spectra_kernel(x_ref, taps_ref, bins_ref, mask_ref, send_ref, fir_ref, table_ref, left_ref, res_ref, dec_ref):
    build_fir(taps_ref, fir_ref)
    build_table(bins_ref, table_ref)
    build_left(x_ref, left_ref)
    res_ref[...] = jnp.dot(left_ref[...], fir_ref[...], preferred_element_type=F32)
    align_windows(res_ref, dec_ref)
    spectrum = jnp.dot(dec_ref[...], table_ref[...], preferred_element_type=F32)
    power = jnp.sum(spectrum * spectrum, axis=1, keepdims=True) / BINS
    channel = iota((80, 8), 0) % ROWS
    live = jnp.broadcast_to(mask_ref[...].astype(F32), (80, 8))
    live = jnp.sum(jnp.where(channel == iota((80, 8), 1), live, 0.0), axis=1, keepdims=True)
    white = spectrum * (lax.rsqrt(power + 1e-06) * live)
    pack(white, send_ref)


def spectra(raw_strain, fir_taps, band_bins, live_mask):
    vmem = pl.BlockSpec(memory_space=pltpu.VMEM)
    return pl.pallas_call(
        spectra_kernel,
        out_shape=jax.ShapeDtypeStruct((4, 16, PACK), BF16),
        in_specs=[vmem] * 4,
        out_specs=vmem,
        scratch_shapes=[
            pltpu.VMEM((SPAN, 256), BF16),
            pltpu.VMEM((NTP, 512), BF16),
            pltpu.VMEM((1024, SPAN), BF16),
            pltpu.VMEM((1024, 256), F32),
            pltpu.VMEM((80, NTP), BF16),
        ],
        compiler_params=pltpu.CompilerParams(vmem_limit_bytes=32 * 1024 * 1024),
        name="spectra",
    )(raw_strain, fir_taps.reshape(1, TAPS), band_bins.reshape(1, BINS), live_mask)


def gather_kernel(send_ref, own_ref, all_ref, raw, hold, z_send, z_recv, g_send, g_recv, local_sem):
    z = lax.axis_index("freq")
    b = lax.axis_index("chan")
    x, y, c = b // 8, (b // 2) % 4, b % 2

    def index(xx, yy, cc):
        return (xx % 4 * 4 + yy % 4) * 2 + cc

    sibling = index(x, y, 1 - c)
    peers = [((z + d) % 4, b) for d in (1, 2, 3)]
    peers += [(z, index(x + d, y, c)) for d in (1, 3)]
    peers += [(z, index(x, y + d, c)) for d in (1, 3)]
    peers += [(z, sibling)]
    barrier = pltpu.get_barrier_semaphore()
    for peer in peers:
        pl.semaphore_signal(barrier, inc=1, device_id=peer, device_id_type=MESH)
    pl.semaphore_wait(barrier, len(peers))

    crossing = []
    for d in (1, 2, 3):
        to = (z + d) % 4
        copy = pltpu.make_async_remote_copy(
            src_ref=send_ref.at[to], dst_ref=raw.at[z],
            send_sem=z_send.at[d - 1], recv_sem=z_recv.at[d - 1],
            device_id=(to, b), device_id_type=MESH,
        )
        copy.start()
        crossing.append(copy)
    raw[z] = send_ref[z]
    for copy in crossing:
        copy.wait_recv()
    for pair in range(2):
        even = raw[2 * pair].astype(F32)
        odd = raw[2 * pair + 1].astype(F32)
        low = jnp.concatenate([even[0:8], odd[0:8]], axis=0).astype(BF16)
        high = jnp.concatenate([even[8:16], odd[8:16]], axis=0).astype(BF16)
        for g in range(5):
            hold[16 * pair : 16 * pair + 16, 256 * g : 256 * g + TILE] = low[:, TILE * g : TILE * g + TILE]
            hold[16 * pair : 16 * pair + 16, 256 * g + TILE : 256 * g + 256] = high[:, TILE * g : TILE * g + TILE]

    own_copy = pltpu.make_async_copy(hold, own_ref, local_sem.at[0])
    own_copy.start()
    own_all = pltpu.make_async_copy(hold, all_ref.at[b], local_sem.at[1])
    own_all.start()

    started = []
    full, first, second = (0, WIDE), (0, WIDE // 2), (WIDE // 2, WIDE // 2)

    def spot(source, half, lanes):
        return all_ref.at[source, pl.ds(16 * half, 16), pl.ds(*lanes)]

    def push(source, half, lanes, target, held=False):
        at = len(started)
        src = hold.at[pl.ds(16 * half, 16), pl.ds(*lanes)] if held else spot(source, half, lanes)
        copy = pltpu.make_async_remote_copy(
            src_ref=src, dst_ref=spot(source, half, lanes),
            send_sem=g_send.at[at], recv_sem=g_recv.at[at],
            device_id=(z, target), device_id_type=MESH,
        )
        copy.start()
        started.append(copy)
        return copy

    def arrived(copy, source, half, lanes):
        copy.wait_recv()

    def near(half, d):
        return index(x + d, y, c) if half == 0 else index(x, y + d, c)

    def far(half, d):
        return index(x, y + d, c) if half == 0 else index(x + d, y, c)

    def block(half, u, v, cc):
        return index(x + u, y + v, cc) if half == 0 else index(x + v, y + u, cc)

    siblings = []

    def share(half, u, v, held=False):
        copy = push(block(half, u, v, c), half, full, sibling, held)
        siblings.append((copy, half, u, v))

    outer = {}

    def spread(half, u, held=False):
        for d in (1, -1):
            outer[half, u, d] = push(block(half, u, 0, c), half, full, far(half, d), held)

    one = {}
    for half in (0, 1):
        for d in (1, -1):
            one[half, d] = push(b, half, full, near(half, d), True)
    for half in (0, 1):
        spread(half, 0, True)
        share(half, 0, 0, True)
    relay = {}
    for half in (0, 1):
        for d in (1, -1):
            source = block(half, -d, 0, c)
            arrived(one[half, d], source, half, full)
            relay[half, d] = push(source, half, first if d == 1 else second, near(half, d))
    for half in (0, 1):
        for d in (1, -1):
            spread(half, -d)
            share(half, -d, 0)
    onward = {}

    def pass_on(half, u):
        for d in (1, -1):
            source = block(half, u, -d, c)
            arrived(outer[half, u, d], source, half, full)
            onward[half, u, d] = push(source, half, first if d == 1 else second, far(half, d))
            share(half, u, -d)

    def finish(half, u):
        source = block(half, u, 2, c)
        arrived(onward[half, u, 1], source, half, first)
        arrived(onward[half, u, -1], source, half, second)
        share(half, u, 2)

    for half in (0, 1):
        source = block(half, 2, 0, c)
        arrived(relay[half, 1], source, half, first)
        arrived(relay[half, -1], source, half, second)
        spread(half, 2)
        share(half, 2, 0)
    for u in (0, -1, 1, 2):
        for half in (0, 1):
            pass_on(half, u)
    for u in (0, -1, 1, 2):
        for half in (0, 1):
            finish(half, u)
    for copy, half, u, v in siblings:
        arrived(copy, block(half, u, v, 1 - c), half, full)
    for copy in started:
        copy.wait_send()
    for copy in crossing:
        copy.wait_send()
    own_copy.wait()
    own_all.wait()


def gather(send):
    vmem = pl.BlockSpec(memory_space=pltpu.VMEM)
    hbm = pl.BlockSpec(memory_space=pl.ANY)
    count = 72
    return pl.pallas_call(
        gather_kernel,
        out_shape=(
            jax.ShapeDtypeStruct((32, WIDE), BF16),
            jax.ShapeDtypeStruct((32, 32, WIDE), BF16),
        ),
        in_specs=[vmem],
        out_specs=(hbm, hbm),
        scratch_shapes=[
            pltpu.VMEM((4, 16, PACK), BF16),
            pltpu.VMEM((32, WIDE), BF16),
            pltpu.SemaphoreType.DMA((3,)),
            pltpu.SemaphoreType.DMA((3,)),
            pltpu.SemaphoreType.DMA((count,)),
            pltpu.SemaphoreType.DMA((count,)),
            pltpu.SemaphoreType.DMA((2,)),
        ],
        compiler_params=pltpu.CompilerParams(
            collective_id=0, has_side_effects=True, vmem_limit_bytes=8 * 1024 * 1024
        ),
        name="gather",
    )(send)


PER_STEP = 4


def correlate_kernel(own_ref, all_ref, out_ref):
    step = pl.program_id(0) % (GROUP // PER_STEP)
    own = own_ref[...].astype(F32)
    lane = iota((32, 256), 1)
    turned = jnp.where(
        lane < 120, pltpu.roll(own, 256 - 120, 1), jnp.where(lane < 240, -pltpu.roll(own, 120, 1), 0.0)
    )
    bin_of = lane % GROUP
    rows = []
    for f in range(PER_STEP):
        keep = bin_of == step * PER_STEP + f
        rows.append(jnp.where(keep, own, 0.0))
        rows.append(jnp.where(keep, turned, 0.0))
    left = jnp.concatenate(rows, axis=0).astype(BF16)
    right = all_ref[...].reshape(1024, 256)
    prod = lax.dot_general(left, right, (((1,), (1,)), ((), ())), preferred_element_type=F32)
    out_ref[...] = (prod * (1.0 / WIN)).reshape(PER_STEP, 2, 32, 1024)


def correlate(own, everyone):
    per_group = GROUP // PER_STEP
    return pl.pallas_call(
        correlate_kernel,
        out_shape=jax.ShapeDtypeStruct((60, 2, 32, 1024), F32),
        grid=(60 // PER_STEP,),
        in_specs=[
            pl.BlockSpec((32, 256), lambda i: (0, i // per_group)),
            pl.BlockSpec((32, 32, 256), lambda i: (0, 0, i // per_group)),
        ],
        out_specs=pl.BlockSpec((PER_STEP, 2, 32, 1024), lambda i: (i, 0, 0, 0)),
        compiler_params=pltpu.CompilerParams(vmem_limit_bytes=32 * 1024 * 1024),
        name="correlate",
    )(own, everyone)


def shards(raw_strain, fir_taps, band_bins, live_mask):
    send = spectra(raw_strain, fir_taps, band_bins, live_mask)
    own, everyone = gather(send)
    return correlate(own, everyone)


def solution(mesh):
    in_specs = (P("chan", "freq", None), P(), P(), P("chan", "freq"))
    out_specs = P("freq", None, "chan", None)
    return jax.shard_map(shards, mesh=mesh, in_specs=in_specs, out_specs=out_specs, check_vma=False)
```

```python
import functools
import math

import jax
import jax.numpy as jnp
from jax import lax
from jax.experimental import pallas as pl
from jax.experimental.pallas import tpu as pltpu
from jax.sharding import PartitionSpec as P

WIN = 10
DECIM = 10
NT = 1500
TAPS = 20
BINS = 240
ROWS = 8
TILE = 128
SPAN = TILE * DECIM
SAMPLES = WIN * NT * DECIM
TILES = -(-SAMPLES // SPAN)
NTP = 12 * TILE
GROUP = 12
PACK = 5 * TILE
WIDE = 5 * 256
F32 = jnp.float32
BF16 = jnp.bfloat16
I32 = jnp.int32
MESH = pl.DeviceIdType.MESH


def iota(shape, axis):
    return lax.broadcasted_iota(I32, shape, axis)


def build_fir(taps_ref, fir_ref):
    row = iota((80, TAPS), 0)
    phase = row % DECIM
    tap = iota((80, TAPS), 1)
    taps = jnp.broadcast_to(taps_ref[...].astype(F32), (80, TAPS))
    near = jnp.sum(jnp.where(tap == 9 - phase, taps, 0.0), axis=1, keepdims=True)
    far = jnp.sum(jnp.where(tap == 19 - phase, taps, 0.0), axis=1, keepdims=True)
    near = jnp.broadcast_to(near, (80, 256))
    far = jnp.broadcast_to(far, (80, 256))
    gap = iota((80, 256), 1) - iota((80, 256), 0) // DECIM
    for step in range(SPAN // 80):
        block = jnp.where(gap == 8 * step, near, jnp.where(gap == 8 * step + 1, far, 0.0))
        fir_ref[80 * step : 80 * step + 80, :] = block.astype(BF16)


def build_table(bins_ref, table_ref):
    bins = bins_ref[...].astype(F32)
    bins = jnp.concatenate([bins, jnp.zeros((1, 16), F32)], axis=1)
    row = iota((40, 256), 0)
    times = jnp.where(row < 8, row, jnp.where(row < 24, 8 * (row - 8), 128 * (row - 24)))
    product = times.astype(F32) * bins
    turns = jnp.floor(product * (1.0 / NT))
    left = product - turns * NT
    left = jnp.where(left < 0, left + NT, left)
    left = jnp.where(left >= NT, left - NT, left)
    angle = left * F32(2.0 * math.pi / NT)
    re = jnp.cos(angle)
    im = -jnp.sin(angle)
    kept = iota((40, 256), 1) < BINS
    re = jnp.where(kept, re, 0.0)
    im = jnp.where(kept, im, 0.0)
    base_re, base_im = [], []
    for b in range(16):
        tr, ti = re[8 + b : 9 + b], im[8 + b : 9 + b]
        base_re.append(re[0:8] * tr - im[0:8] * ti)
        base_im.append(re[0:8] * ti + im[0:8] * tr)
    base_re = jnp.concatenate(base_re, axis=0)
    base_im = jnp.concatenate(base_im, axis=0)
    for a in range(12):
        tr, ti = re[24 + a : 25 + a], im[24 + a : 25 + a]
        block_re = base_re * tr - base_im * ti
        block_im = base_re * ti + base_im * tr
        if a == 11:
            inside = iota((TILE, 256), 0) < NT - 11 * TILE
            block_re = jnp.where(inside, block_re, 0.0)
            block_im = jnp.where(inside, block_im, 0.0)
        table_ref[TILE * a : TILE * a + TILE, 0:256] = block_re.astype(BF16)
        table_ref[TILE * a : TILE * a + TILE, 256:512] = block_im.astype(BF16)


def build_left(x_ref, left_ref):
    def tile(t):
        return x_ref[0, :, SPAN * t : min(SPAN * t + SPAN, SAMPLES)].astype(F32)

    blocks = [(t, None) for t in range(TILES)]
    for w in range(1, WIN):
        t = NT * w // TILE
        blocks.append((t, NT * DECIM * w - SPAN * t))
    blocks.append((None, None))

    def value(block):
        t, first = block
        if t is None:
            return jnp.zeros((ROWS, SPAN), F32)
        part = tile(t)
        if part.shape[1] < SPAN:
            part = jnp.concatenate([part, jnp.zeros((ROWS, SPAN - part.shape[1]), F32)], axis=1)
        if first is not None:
            part = jnp.where(iota((ROWS, SPAN), 1) < first, 0.0, part)
        return part

    for pair in range(len(blocks) // 2):
        both = jnp.concatenate([value(blocks[2 * pair]), value(blocks[2 * pair + 1])], axis=0)
        left_ref[16 * pair : 16 * pair + 16, :] = both.astype(BF16)


def align_windows(res_ref, dec_ref):
    lane = iota((ROWS, TILE), 1)

    def plain(t):
        main = res_ref[8 * t : 8 * t + 8, 0:TILE]
        if t == 0:
            return main
        return main + res_ref[8 * t - 8 : 8 * t, TILE : 2 * TILE]

    def window(w):
        t = NT * w // TILE
        shift = NT * w - TILE * t
        tiles = [plain(t + u) for u in range(1, 13 if shift else 12)]
        if w == 0:
            first = plain(0)
        else:
            at = 8 * (TILES + w - 1)
            first = res_ref[at : at + 8, 0:TILE]
        tiles = [first] + tiles
        if shift:
            rolled = [pltpu.roll(one, TILE - shift, 1) for one in tiles]
            tiles = [
                jnp.where(lane < TILE - shift, rolled[u], rolled[u + 1]) for u in range(12)
            ]
        return jnp.concatenate(tiles, axis=1)

    for pair in range(WIN // 2):
        both = jnp.concatenate([window(2 * pair), window(2 * pair + 1)], axis=0)
        dec_ref[16 * pair : 16 * pair + 16, :] = both.astype(BF16)


def pack(white, send_ref):
    lane = iota((ROWS, 256), 1)
    segment = lane // GROUP
    wrapped = (lane + 256) // GROUP
    turned = []
    for part in range(2):
        for w in range(WIN):
            spot = part * WIN + w
            piece = white[8 * w : 8 * w + 8, 256 * part : 256 * part + 256]
            turned.append(pltpu.roll(piece, GROUP * spot, 1) if spot else piece)
    for group in range(BINS // GROUP):
        halves = []
        for half in range(2):
            lanes = slice(TILE * half, TILE * half + TILE)
            total = jnp.zeros((ROWS, TILE), F32)
            for spot in range(2 * WIN):
                start = GROUP * (spot + group)
                covers = [
                    at
                    for at in (start, start - 256)
                    if at < TILE * half + TILE and at + GROUP > TILE * half
                ]
                for at in covers:
                    ids = segment if at == start else wrapped
                    total = jnp.where(
                        ids[:, lanes] == spot + group, turned[spot][:, lanes], total
                    )
            halves.append(total)
        dest = jnp.concatenate(halves, axis=1)
        if group:
            dest = pltpu.roll(dest, 256 - GROUP * group, 1)
        both = jnp.concatenate([dest[:, 0:TILE], dest[:, TILE:256]], axis=0)
        z, g = group // 5, group % 5
        send_ref[z, :, TILE * g : TILE * g + TILE] = both.astype(BF16)


def spectra(x_ref, loaded, taps_ref, bins_ref, mask_ref, send_ref, fir_ref, table_ref, left_ref, res_ref, dec_ref):
    build_fir(taps_ref, fir_ref)
    build_table(bins_ref, table_ref)
    loaded.wait()
    build_left(x_ref, left_ref)
    res_ref[...] = jnp.dot(left_ref[...], fir_ref[...], preferred_element_type=F32)
    align_windows(res_ref, dec_ref)
    spectrum = jnp.dot(dec_ref[...], table_ref[...], preferred_element_type=F32)
    power = jnp.sum(spectrum * spectrum, axis=1, keepdims=True) / BINS
    channel = iota((80, 8), 0) % ROWS
    live = jnp.broadcast_to(mask_ref[...].astype(F32), (80, 8))
    live = jnp.sum(jnp.where(channel == iota((80, 8), 1), live, 0.0), axis=1, keepdims=True)
    white = spectrum * (lax.rsqrt(power + 1e-06) * live)
    pack(white, send_ref)


PROGRAM = (
    ("s", 1), ("s", -1), ("s", 2), ("S", 0, 1), ("S", 0, -1), ("H", 0, 0),
    ("w", 1), ("S", -1, 1), ("S", -1, -1), ("w", -1), ("S", 1, 1), ("S", 1, -1), ("H", -1, 0), ("H", 1, 0),
    ("w", 2), ("S", 2, 1), ("S", 2, -1), ("S", 2, 2), ("S", -1, 2), ("S", 1, 2), ("H", 2, 0),
    ("W", 0, 1), ("R", 0, 1), ("W", 0, -1), ("R", 0, -1), ("H", 0, -1), ("H", 0, 1),
    ("W", -1, 1), ("H", -1, -1), ("W", -1, -1), ("H", -1, 1),
    ("W", 1, 1), ("H", 1, -1), ("W", 1, -1), ("H", 1, 1),
    ("W", 2, 1), ("H", 2, -1), ("W", 2, -1), ("H", 2, 1),
    ("Q", 0), ("H", 0, 2), ("W", 2, 2), ("H", 2, 2), ("W", -1, 2), ("H", -1, 2), ("W", 1, 2), ("H", 1, 2),
)
COPIES = 2 * sum(step[0] in "sSRH" for step in PROGRAM)


def gather_kernel(
    x_ref, taps_ref, bins_ref, mask_ref, own_ref, all_ref,
    x_here, taps_here, bins_here, mask_here, fir_ref, table_ref, left_ref, res_ref, dec_ref, send_ref, raw,
    in_sem, z_send, z_recv, g_send, g_recv,
):
    z = lax.axis_index("freq")
    b = lax.axis_index("chan")
    x, y, c = b // 8, (b // 2) % 4, b % 2

    def index(xx, yy, cc):
        return (xx % 4 * 4 + yy % 4) * 2 + cc

    sibling = index(x, y, 1 - c)
    peers = [((z + d) % 4, b) for d in (1, 2, 3)]
    peers += [(z, index(x + d, y, c)) for d in (1, 2, 3)]
    peers += [(z, index(x, y + d, c)) for d in (1, 2, 3)]
    peers += [(z, sibling)]
    barrier = pltpu.get_barrier_semaphore()
    for peer in peers:
        pl.semaphore_signal(barrier, inc=1, device_id=peer, device_id_type=MESH)

    small = []
    for at, (src, dst) in enumerate(((taps_ref, taps_here), (bins_ref, bins_here), (mask_ref, mask_here))):
        copy = pltpu.make_async_copy(src, dst, in_sem.at[at])
        copy.start()
        small.append(copy)
    loaded = pltpu.make_async_copy(x_ref, x_here, in_sem.at[3])
    loaded.start()
    for copy in small:
        copy.wait()
    spectra(
        x_here, loaded, taps_here, bins_here, mask_here, send_ref,
        fir_ref, table_ref, left_ref, res_ref, dec_ref,
    )
    pl.semaphore_wait(barrier, len(peers))

    crossing = []
    for d in (2, 1, 3):
        to = (z + d) % 4
        copy = pltpu.make_async_remote_copy(
            src_ref=send_ref.at[to], dst_ref=raw.at[z],
            send_sem=z_send.at[d - 1], recv_sem=z_recv.at[d - 1],
            device_id=(to, b), device_id_type=MESH,
        )
        copy.start()
        crossing.append(copy)
    raw[z] = send_ref[z]
    for copy in crossing:
        copy.wait_recv()
    for pair in range(2):
        rows = slice(16 * pair, 16 * pair + 16)
        even = raw[2 * pair].astype(F32)
        odd = raw[2 * pair + 1].astype(F32)
        low = jnp.concatenate([even[0:8], odd[0:8]], axis=0).astype(BF16)
        high = jnp.concatenate([even[8:16], odd[8:16]], axis=0).astype(BF16)
        for at in range(10):
            source = high if at % 2 else low
            piece = source[:, TILE * (at // 2) : TILE * (at // 2) + TILE]
            lanes = slice(TILE * at, TILE * at + TILE)
            own_ref[rows, lanes] = piece
            all_ref[b, rows, lanes] = piece

    started = []
    full, first, second = (0, WIDE), (0, WIDE // 2), (WIDE // 2, WIDE // 2)

    def push(source, half, lanes, target):
        at = len(started)
        spot = all_ref.at[source, pl.ds(16 * half, 16), pl.ds(*lanes)]
        copy = pltpu.make_async_remote_copy(
            src_ref=spot, dst_ref=spot, send_sem=g_send.at[at], recv_sem=g_recv.at[at],
            device_id=(z, target), device_id_type=MESH,
        )
        copy.start()
        started.append(copy)
        return copy

    def block(half, u, v):
        return index(x + u, y + v, c) if half == 0 else index(x + v, y + u, c)

    def relayed(d):
        return first if d == 1 else second

    near, far, onward, shares = {}, {}, {}, []
    for kind, *args in PROGRAM:
        for half in (0, 1):
            if kind == "s":
                near[half, args[0]] = push(b, half, full, block(half, args[0], 0))
            elif kind == "w":
                near[half, args[0]].wait_recv()
            elif kind == "S":
                u, d = args
                far[half, u, d] = push(block(half, u, 0), half, full, block(half, 0, d))
            elif kind == "W":
                far[(half, *args)].wait_recv()
            elif kind == "R":
                u, d = args
                onward[half, u, d] = push(block(half, u, -d), half, relayed(d), block(half, 0, d))
            elif kind == "Q":
                onward[half, args[0], 1].wait_recv()
                onward[half, args[0], -1].wait_recv()
            else:
                shares.append(push(block(half, *args), half, full, sibling))
    for copy in shares:
        copy.wait_recv()
    for copy in started + crossing:
        copy.wait_send()


def gather(raw_strain, fir_taps, band_bins, live_mask):
    vmem = pl.BlockSpec(memory_space=pltpu.VMEM)
    hbm = pl.BlockSpec(memory_space=pltpu.HBM)
    arrays = (raw_strain, fir_taps.reshape(1, TAPS), band_bins.reshape(1, BINS), live_mask)
    arrays = [pltpu.with_memory_space_constraint(one, pltpu.HBM) for one in arrays]
    return pl.pallas_call(
        gather_kernel,
        out_shape=(
            jax.ShapeDtypeStruct((32, WIDE), BF16),
            jax.ShapeDtypeStruct((32, 32, WIDE), BF16),
        ),
        in_specs=[hbm] * 4,
        out_specs=(vmem, vmem),
        scratch_shapes=[
            pltpu.VMEM((1, ROWS, SAMPLES), BF16),
            pltpu.VMEM((1, TAPS), BF16),
            pltpu.VMEM((1, BINS), I32),
            pltpu.VMEM((1, 8), I32),
            pltpu.VMEM((SPAN, 256), BF16),
            pltpu.VMEM((NTP, 512), BF16),
            pltpu.VMEM((1024, SPAN), BF16),
            pltpu.VMEM((1024, 256), F32),
            pltpu.VMEM((80, NTP), BF16),
            pltpu.VMEM((4, 16, PACK), BF16),
            pltpu.VMEM((4, 16, PACK), BF16),
            pltpu.SemaphoreType.DMA((4,)),
            pltpu.SemaphoreType.DMA((3,)),
            pltpu.SemaphoreType.DMA((3,)),
            pltpu.SemaphoreType.DMA((COPIES,)),
            pltpu.SemaphoreType.DMA((COPIES,)),
        ],
        compiler_params=pltpu.CompilerParams(
            collective_id=0, has_side_effects=True, vmem_limit_bytes=32 * 1024 * 1024
        ),
        name="gather",
    )(*arrays)


SLOTS = 8


def correlate_kernel(own_ref, all_ref, out_ref, left_ref, slot_ref, sem):
    lane = iota((32, 256), 1)
    copies = []
    for g in range(5):
        lanes = slice(256 * g, 256 * g + 256)
        own = own_ref[:, lanes].astype(F32)
        turned = jnp.where(
            lane < 120,
            pltpu.roll(own, 256 - 120, 1),
            jnp.where(lane < 240, -pltpu.roll(own, 120, 1), 0.0),
        )
        for f in range(GROUP):
            keep = lane % GROUP == f
            both = jnp.concatenate([jnp.where(keep, own, 0.0), jnp.where(keep, turned, 0.0)], axis=0)
            left_ref[64 * f : 64 * f + 64, :] = both.astype(BF16)
        for part in range(4):
            at = len(copies)
            slot = at % SLOTS
            if at >= SLOTS:
                copies[at - SLOTS].wait()
            right = all_ref[8 * part : 8 * part + 8, :, lanes].reshape(256, 256)
            prod = lax.dot_general(
                left_ref[...], right, (((1,), (1,)), ((), ())), preferred_element_type=F32
            )
            slot_ref[slot] = (prod * (1.0 / WIN)).reshape(GROUP, 2, 32, 256)
            copy = pltpu.make_async_copy(
                slot_ref.at[slot],
                out_ref.at[pl.ds(GROUP * g, GROUP), :, :, pl.ds(256 * part, 256)],
                sem.at[slot],
            )
            copy.start()
            copies.append(copy)
    for copy in copies[-SLOTS:]:
        copy.wait()


def correlate(own, everyone):
    vmem = pl.BlockSpec(memory_space=pltpu.VMEM)
    return pl.pallas_call(
        correlate_kernel,
        out_shape=jax.ShapeDtypeStruct((60, 2, 32, 1024), F32),
        in_specs=[vmem, vmem],
        out_specs=pl.BlockSpec(memory_space=pltpu.HBM),
        scratch_shapes=[
            pltpu.VMEM((64 * GROUP, 256), BF16),
            pltpu.VMEM((SLOTS, GROUP, 2, 32, 256), F32),
            pltpu.SemaphoreType.DMA((SLOTS,)),
        ],
        compiler_params=pltpu.CompilerParams(vmem_limit_bytes=32 * 1024 * 1024),
        name="correlate",
    )(own, everyone)


def shards(raw_strain, fir_taps, band_bins, live_mask):
    own, everyone = gather(raw_strain, fir_taps, band_bins, live_mask)
    return correlate(own, everyone)


def solution(mesh):
    in_specs = (P("chan", "freq", None), P(), P(), P("chan", "freq"))
    out_specs = P("freq", None, "chan", None)
    return jax.shard_map(shards, mesh=mesh, in_specs=in_specs, out_specs=out_specs, check_vma=False)
```

```python
import functools
import math

import jax
import jax.numpy as jnp
from jax import lax
from jax.experimental import pallas as pl
from jax.experimental.pallas import tpu as pltpu
from jax.sharding import PartitionSpec as P

WIN = 10
DECIM = 10
NT = 1500
TAPS = 20
BINS = 240
ROWS = 8
TILE = 128
SPAN = TILE * DECIM
SAMPLES = WIN * NT * DECIM
TILES = -(-SAMPLES // SPAN)
NTP = 12 * TILE
GROUP = 12
PACK = 5 * TILE
WIDE = 5 * 256
F32 = jnp.float32
BF16 = jnp.bfloat16
I32 = jnp.int32
MESH = pl.DeviceIdType.MESH


def iota(shape, axis):
    return lax.broadcasted_iota(I32, shape, axis)


def build_fir(taps_ref, fir_ref):
    row = iota((80, TAPS), 0)
    phase = row % DECIM
    tap = iota((80, TAPS), 1)
    taps = jnp.broadcast_to(taps_ref[...].astype(F32), (80, TAPS))
    near = jnp.sum(jnp.where(tap == 9 - phase, taps, 0.0), axis=1, keepdims=True)
    far = jnp.sum(jnp.where(tap == 19 - phase, taps, 0.0), axis=1, keepdims=True)
    near = jnp.broadcast_to(near, (80, 256))
    far = jnp.broadcast_to(far, (80, 256))
    gap = iota((80, 256), 1) - iota((80, 256), 0) // DECIM
    for step in range(SPAN // 80):
        block = jnp.where(gap == 8 * step, near, jnp.where(gap == 8 * step + 1, far, 0.0))
        fir_ref[80 * step : 80 * step + 80, :] = block.astype(BF16)


def build_table(bins_ref, table_ref):
    bins = bins_ref[...].astype(F32)
    bins = jnp.concatenate([bins, jnp.zeros((1, 16), F32)], axis=1)
    row = iota((40, 256), 0)
    times = jnp.where(row < 8, row, jnp.where(row < 24, 8 * (row - 8), 128 * (row - 24)))
    product = times.astype(F32) * bins
    turns = jnp.floor(product * (1.0 / NT))
    left = product - turns * NT
    left = jnp.where(left < 0, left + NT, left)
    left = jnp.where(left >= NT, left - NT, left)
    angle = left * F32(2.0 * math.pi / NT)
    re = jnp.cos(angle)
    im = -jnp.sin(angle)
    kept = iota((40, 256), 1) < BINS
    re = jnp.where(kept, re, 0.0)
    im = jnp.where(kept, im, 0.0)
    base_re, base_im = [], []
    for b in range(16):
        tr, ti = re[8 + b : 9 + b], im[8 + b : 9 + b]
        base_re.append(re[0:8] * tr - im[0:8] * ti)
        base_im.append(re[0:8] * ti + im[0:8] * tr)
    base_re = jnp.concatenate(base_re, axis=0)
    base_im = jnp.concatenate(base_im, axis=0)
    for a in range(12):
        tr, ti = re[24 + a : 25 + a], im[24 + a : 25 + a]
        block_re = base_re * tr - base_im * ti
        block_im = base_re * ti + base_im * tr
        if a == 11:
            inside = iota((TILE, 256), 0) < NT - 11 * TILE
            block_re = jnp.where(inside, block_re, 0.0)
            block_im = jnp.where(inside, block_im, 0.0)
        table_ref[TILE * a : TILE * a + TILE, 0:256] = block_re.astype(BF16)
        table_ref[TILE * a : TILE * a + TILE, 256:512] = block_im.astype(BF16)


def build_left(x_ref, left_ref):
    def tile(t):
        return x_ref[0, :, SPAN * t : min(SPAN * t + SPAN, SAMPLES)].astype(F32)

    blocks = [(t, None) for t in range(TILES)]
    for w in range(1, WIN):
        t = NT * w // TILE
        blocks.append((t, NT * DECIM * w - SPAN * t))
    blocks.append((None, None))

    def value(block):
        t, first = block
        if t is None:
            return jnp.zeros((ROWS, SPAN), F32)
        part = tile(t)
        if part.shape[1] < SPAN:
            part = jnp.concatenate([part, jnp.zeros((ROWS, SPAN - part.shape[1]), F32)], axis=1)
        if first is not None:
            part = jnp.where(iota((ROWS, SPAN), 1) < first, 0.0, part)
        return part

    for pair in range(len(blocks) // 2):
        both = jnp.concatenate([value(blocks[2 * pair]), value(blocks[2 * pair + 1])], axis=0)
        left_ref[16 * pair : 16 * pair + 16, :] = both.astype(BF16)


def align_windows(res_ref, dec_ref):
    lane = iota((ROWS, TILE), 1)

    def plain(t):
        main = res_ref[8 * t : 8 * t + 8, 0:TILE]
        if t == 0:
            return main
        return main + res_ref[8 * t - 8 : 8 * t, TILE : 2 * TILE]

    def window(w):
        t = NT * w // TILE
        shift = NT * w - TILE * t
        tiles = [plain(t + u) for u in range(1, 13 if shift else 12)]
        if w == 0:
            first = plain(0)
        else:
            at = 8 * (TILES + w - 1)
            first = res_ref[at : at + 8, 0:TILE]
        tiles = [first] + tiles
        if shift:
            rolled = [pltpu.roll(one, TILE - shift, 1) for one in tiles]
            tiles = [
                jnp.where(lane < TILE - shift, rolled[u], rolled[u + 1]) for u in range(12)
            ]
        return jnp.concatenate(tiles, axis=1)

    for pair in range(WIN // 2):
        both = jnp.concatenate([window(2 * pair), window(2 * pair + 1)], axis=0)
        dec_ref[16 * pair : 16 * pair + 16, :] = both.astype(BF16)


def pack(white, send_ref):
    lane = iota((ROWS, 256), 1)
    segment = lane // GROUP
    wrapped = (lane + 256) // GROUP
    turned = []
    for part in range(2):
        for w in range(WIN):
            spot = part * WIN + w
            piece = white[8 * w : 8 * w + 8, 256 * part : 256 * part + 256]
            turned.append(pltpu.roll(piece, GROUP * spot, 1) if spot else piece)
    for group in range(BINS // GROUP):
        halves = []
        for half in range(2):
            lanes = slice(TILE * half, TILE * half + TILE)
            total = jnp.zeros((ROWS, TILE), F32)
            for spot in range(2 * WIN):
                start = GROUP * (spot + group)
                covers = [
                    at
                    for at in (start, start - 256)
                    if at < TILE * half + TILE and at + GROUP > TILE * half
                ]
                for at in covers:
                    ids = segment if at == start else wrapped
                    total = jnp.where(
                        ids[:, lanes] == spot + group, turned[spot][:, lanes], total
                    )
            halves.append(total)
        dest = jnp.concatenate(halves, axis=1)
        if group:
            dest = pltpu.roll(dest, 256 - GROUP * group, 1)
        both = jnp.concatenate([dest[:, 0:TILE], dest[:, TILE:256]], axis=0)
        z, g = group // 5, group % 5
        send_ref[z, :, TILE * g : TILE * g + TILE] = both.astype(BF16)


def spectra(x_ref, loaded, taps_ref, bins_ref, mask_ref, send_ref, fir_ref, table_ref, left_ref, res_ref, dec_ref):
    build_fir(taps_ref, fir_ref)
    build_table(bins_ref, table_ref)
    loaded.wait()
    build_left(x_ref, left_ref)
    res_ref[...] = jnp.dot(left_ref[...], fir_ref[...], preferred_element_type=F32)
    align_windows(res_ref, dec_ref)
    spectrum = jnp.dot(dec_ref[...], table_ref[...], preferred_element_type=F32)
    power = jnp.sum(spectrum * spectrum, axis=1, keepdims=True) / BINS
    channel = iota((80, 8), 0) % ROWS
    live = jnp.broadcast_to(mask_ref[...].astype(F32), (80, 8))
    live = jnp.sum(jnp.where(channel == iota((80, 8), 1), live, 0.0), axis=1, keepdims=True)
    white = spectrum * (lax.rsqrt(power + 1e-06) * live)
    pack(white, send_ref)


COPIES = 4 * (3 + 12 + 4)


def gather_kernel(
    x_ref, taps_ref, bins_ref, mask_ref, own_ref, all_ref,
    x_here, taps_here, bins_here, mask_here, fir_ref, table_ref, left_ref, res_ref, dec_ref, send_ref, raw,
    in_sem, z_send, z_recv, g_send, g_recv,
):
    z = lax.axis_index("freq")
    b = lax.axis_index("chan")
    x, y, c = b // 8, (b // 2) % 4, b % 2

    def index(xx, yy, cc):
        return (xx % 4 * 4 + yy % 4) * 2 + cc

    sibling = index(x, y, 1 - c)
    peers = [((z + d) % 4, b) for d in (1, 2, 3)]
    peers += [(z, index(x + d, y, c)) for d in (1, 2, 3)]
    peers += [(z, index(x, y + d, c)) for d in (1, 2, 3)]
    peers += [(z, sibling)]
    barrier = pltpu.get_barrier_semaphore()
    for peer in peers:
        pl.semaphore_signal(barrier, inc=1, device_id=peer, device_id_type=MESH)

    small = []
    for at, (src, dst) in enumerate(((taps_ref, taps_here), (bins_ref, bins_here), (mask_ref, mask_here))):
        copy = pltpu.make_async_copy(src, dst, in_sem.at[at])
        copy.start()
        small.append(copy)
    loaded = pltpu.make_async_copy(x_ref, x_here, in_sem.at[3])
    loaded.start()
    for copy in small:
        copy.wait()
    spectra(
        x_here, loaded, taps_here, bins_here, mask_here, send_ref,
        fir_ref, table_ref, left_ref, res_ref, dec_ref,
    )
    pl.semaphore_wait(barrier, len(peers))

    crossing, landed = [], {}
    for d in (2, 1, 3):
        to = (z + d) % 4
        copy = pltpu.make_async_remote_copy(
            src_ref=send_ref.at[to], dst_ref=raw.at[z],
            send_sem=z_send.at[d - 1], recv_sem=z_recv.at[d - 1],
            device_id=(to, b), device_id_type=MESH,
        )
        copy.start()
        crossing.append(copy)
        landed[d] = copy
    raw[z] = send_ref[z]

    started, shares = [], []

    def push(region, target):
        at = len(started)
        copy = pltpu.make_async_remote_copy(
            src_ref=region, dst_ref=region, send_sem=g_send.at[at], recv_sem=g_recv.at[at],
            device_id=(z, target), device_id_type=MESH,
        )
        copy.start()
        started.append(copy)
        return copy

    def place(route, u, v):
        return ((x + u) % 4, (y + v) % 4) if route == 0 else ((x + v) % 4, (y + u) % 4)

    def part(half, route):
        return pl.ds(16 * half, 16), pl.ds(PACK * route, PACK)

    def send(half, route, u, u_to, v_to):
        xx, yy = place(route, u, 0)
        region = all_ref.at[(xx, yy, c) + part(half, route)]
        return push(region, index(*place(route, u_to, v_to), c))

    def share(half, route, u):
        xx, yy = place(route, u, 0)
        if route == 0:
            region = all_ref.at[(xx, slice(None), c) + part(half, route)]
        else:
            region = all_ref.at[(slice(None), yy, c) + part(half, route)]
        shares.append(push(region, sibling))

    near, far = {}, {}

    def unite(half):
        rows = slice(16 * half, 16 * half + 16)
        even = raw[2 * half].astype(F32)
        odd = raw[2 * half + 1].astype(F32)
        low = jnp.concatenate([even[0:8], odd[0:8]], axis=0).astype(BF16)
        high = jnp.concatenate([even[8:16], odd[8:16]], axis=0).astype(BF16)
        for at in range(10):
            source = high if at % 2 else low
            piece = source[:, TILE * (at // 2) : TILE * (at // 2) + TILE]
            lanes = slice(TILE * at, TILE * at + TILE)
            own_ref[rows, lanes] = piece
            all_ref[x, y, c, rows, lanes] = piece

    def begin(half):
        for d in (1, -1, 2):
            for route in (0, 1):
                near[half, route, d] = send(half, route, 0, d, 0)
        for d in (1, -1, 2):
            for route in (0, 1):
                far[half, route, 0, d] = send(half, route, 0, 0, d)

    def go_on(half):
        for d in (1, -1, 2):
            u = d if d == 2 else -d
            for route in (0, 1):
                near[half, route, d].wait_recv()
                for v in (1, -1, 2):
                    far[half, route, u, v] = send(half, route, u, 0, v)

    def finish(half):
        for u in (0, -1, 1, 2):
            for route in (0, 1):
                for v in (1, -1, 2):
                    far[half, route, u, v].wait_recv()
                share(half, route, u)

    def arrive(source):
        for d in (1, 2, 3):
            @pl.when((z - source + 4) % 4 == d)
            def _():
                landed[d].wait_recv()

    arrive(0)
    arrive(1)
    unite(0)
    begin(0)
    arrive(2)
    arrive(3)
    unite(1)
    begin(1)
    go_on(0)
    go_on(1)
    finish(0)
    finish(1)
    for copy in shares:
        copy.wait_recv()
    for copy in started + crossing:
        copy.wait_send()


def gather(raw_strain, fir_taps, band_bins, live_mask):
    vmem = pl.BlockSpec(memory_space=pltpu.VMEM)
    hbm = pl.BlockSpec(memory_space=pltpu.HBM)
    arrays = (raw_strain, fir_taps.reshape(1, TAPS), band_bins.reshape(1, BINS), live_mask)
    arrays = [pltpu.with_memory_space_constraint(one, pltpu.HBM) for one in arrays]
    return pl.pallas_call(
        gather_kernel,
        out_shape=(
            jax.ShapeDtypeStruct((32, WIDE), BF16),
            jax.ShapeDtypeStruct((4, 4, 2, 32, WIDE), BF16),
        ),
        in_specs=[hbm] * 4,
        out_specs=(vmem, vmem),
        scratch_shapes=[
            pltpu.VMEM((1, ROWS, SAMPLES), BF16),
            pltpu.VMEM((1, TAPS), BF16),
            pltpu.VMEM((1, BINS), I32),
            pltpu.VMEM((1, 8), I32),
            pltpu.VMEM((SPAN, 256), BF16),
            pltpu.VMEM((NTP, 512), BF16),
            pltpu.VMEM((1024, SPAN), BF16),
            pltpu.VMEM((1024, 256), F32),
            pltpu.VMEM((80, NTP), BF16),
            pltpu.VMEM((4, 16, PACK), BF16),
            pltpu.VMEM((4, 16, PACK), BF16),
            pltpu.SemaphoreType.DMA((4,)),
            pltpu.SemaphoreType.DMA((3,)),
            pltpu.SemaphoreType.DMA((3,)),
            pltpu.SemaphoreType.DMA((COPIES,)),
            pltpu.SemaphoreType.DMA((COPIES,)),
        ],
        compiler_params=pltpu.CompilerParams(
            collective_id=0, has_side_effects=True, vmem_limit_bytes=32 * 1024 * 1024
        ),
        name="gather",
    )(*arrays)


SLOTS = 8


def correlate_kernel(own_ref, all_ref, out_ref, left_ref, slot_ref, sem):
    lane = iota((32, 256), 1)
    copies = []
    for g in range(5):
        lanes = slice(256 * g, 256 * g + 256)
        own = own_ref[:, lanes].astype(F32)
        turned = jnp.where(
            lane < 120,
            pltpu.roll(own, 256 - 120, 1),
            jnp.where(lane < 240, -pltpu.roll(own, 120, 1), 0.0),
        )
        for f in range(GROUP):
            keep = lane % GROUP == f
            both = jnp.concatenate([jnp.where(keep, own, 0.0), jnp.where(keep, turned, 0.0)], axis=0)
            left_ref[64 * f : 64 * f + 64, :] = both.astype(BF16)
        for part in range(4):
            at = len(copies)
            slot = at % SLOTS
            if at >= SLOTS:
                copies[at - SLOTS].wait()
            right = all_ref[8 * part : 8 * part + 8, :, lanes].reshape(256, 256)
            prod = lax.dot_general(
                left_ref[...], right, (((1,), (1,)), ((), ())), preferred_element_type=F32
            )
            slot_ref[slot] = (prod * (1.0 / WIN)).reshape(GROUP, 2, 32, 256)
            copy = pltpu.make_async_copy(
                slot_ref.at[slot],
                out_ref.at[pl.ds(GROUP * g, GROUP), :, :, pl.ds(256 * part, 256)],
                sem.at[slot],
            )
            copy.start()
            copies.append(copy)
    for copy in copies[-SLOTS:]:
        copy.wait()


def correlate(own, everyone):
    vmem = pl.BlockSpec(memory_space=pltpu.VMEM)
    return pl.pallas_call(
        correlate_kernel,
        out_shape=jax.ShapeDtypeStruct((60, 2, 32, 1024), F32),
        in_specs=[vmem, vmem],
        out_specs=pl.BlockSpec(memory_space=pltpu.HBM),
        scratch_shapes=[
            pltpu.VMEM((64 * GROUP, 256), BF16),
            pltpu.VMEM((SLOTS, GROUP, 2, 32, 256), F32),
            pltpu.SemaphoreType.DMA((SLOTS,)),
        ],
        compiler_params=pltpu.CompilerParams(vmem_limit_bytes=32 * 1024 * 1024),
        name="correlate",
    )(own, everyone)


def shards(raw_strain, fir_taps, band_bins, live_mask):
    own, everyone = gather(raw_strain, fir_taps, band_bins, live_mask)
    return correlate(own, everyone.reshape(32, 32, WIDE))


def solution(mesh):
    in_specs = (P("chan", "freq", None), P(), P(), P("chan", "freq"))
    out_specs = P("freq", None, "chan", None)
    return jax.shard_map(shards, mesh=mesh, in_specs=in_specs, out_specs=out_specs, check_vma=False)
```

```python
import functools
import math

import jax
import jax.numpy as jnp
from jax import lax
from jax.experimental import pallas as pl
from jax.experimental.pallas import tpu as pltpu
from jax.sharding import PartitionSpec as P

WIN = 10
DECIM = 10
NT = 1500
TAPS = 20
BINS = 240
ROWS = 8
TILE = 128
SPAN = TILE * DECIM
SAMPLES = WIN * NT * DECIM
TILES = -(-SAMPLES // SPAN)
NTP = 12 * TILE
GROUP = 12
PACK = 5 * TILE
WIDE = 5 * 256
F32 = jnp.float32
BF16 = jnp.bfloat16
I32 = jnp.int32
MESH = pl.DeviceIdType.MESH


def iota(shape, axis):
    return lax.broadcasted_iota(I32, shape, axis)


def build_fir(taps_ref, fir_ref):
    row = iota((80, TAPS), 0)
    phase = row % DECIM
    tap = iota((80, TAPS), 1)
    taps = jnp.broadcast_to(taps_ref[...].astype(F32), (80, TAPS))
    near = jnp.sum(jnp.where(tap == 9 - phase, taps, 0.0), axis=1, keepdims=True)
    far = jnp.sum(jnp.where(tap == 19 - phase, taps, 0.0), axis=1, keepdims=True)
    near = jnp.broadcast_to(near, (80, 256))
    far = jnp.broadcast_to(far, (80, 256))
    gap = iota((80, 256), 1) - iota((80, 256), 0) // DECIM
    for step in range(SPAN // 80):
        block = jnp.where(gap == 8 * step, near, jnp.where(gap == 8 * step + 1, far, 0.0))
        fir_ref[80 * step : 80 * step + 80, :] = block.astype(BF16)


def build_table(bins_ref, table_ref):
    bins = bins_ref[...].astype(F32)
    bins = jnp.concatenate([bins, jnp.zeros((1, 16), F32)], axis=1)
    row = iota((40, 256), 0)
    times = jnp.where(row < 8, row, jnp.where(row < 24, 8 * (row - 8), 128 * (row - 24)))
    product = times.astype(F32) * bins
    turns = jnp.floor(product * (1.0 / NT))
    left = product - turns * NT
    left = jnp.where(left < 0, left + NT, left)
    left = jnp.where(left >= NT, left - NT, left)
    angle = left * F32(2.0 * math.pi / NT)
    re = jnp.cos(angle)
    im = -jnp.sin(angle)
    kept = iota((40, 256), 1) < BINS
    re = jnp.where(kept, re, 0.0)
    im = jnp.where(kept, im, 0.0)
    base_re, base_im = [], []
    for b in range(16):
        tr, ti = re[8 + b : 9 + b], im[8 + b : 9 + b]
        base_re.append(re[0:8] * tr - im[0:8] * ti)
        base_im.append(re[0:8] * ti + im[0:8] * tr)
    base_re = jnp.concatenate(base_re, axis=0)
    base_im = jnp.concatenate(base_im, axis=0)
    for a in range(12):
        tr, ti = re[24 + a : 25 + a], im[24 + a : 25 + a]
        block_re = base_re * tr - base_im * ti
        block_im = base_re * ti + base_im * tr
        if a == 11:
            inside = iota((TILE, 256), 0) < NT - 11 * TILE
            block_re = jnp.where(inside, block_re, 0.0)
            block_im = jnp.where(inside, block_im, 0.0)
        table_ref[TILE * a : TILE * a + TILE, 0:256] = block_re.astype(BF16)
        table_ref[TILE * a : TILE * a + TILE, 256:512] = block_im.astype(BF16)


def build_left(x_ref, left_ref):
    def tile(t):
        return x_ref[0, :, SPAN * t : min(SPAN * t + SPAN, SAMPLES)].astype(F32)

    blocks = [(t, None) for t in range(TILES)]
    for w in range(1, WIN):
        t = NT * w // TILE
        blocks.append((t, NT * DECIM * w - SPAN * t))
    blocks.append((None, None))

    def value(block):
        t, first = block
        if t is None:
            return jnp.zeros((ROWS, SPAN), F32)
        part = tile(t)
        if part.shape[1] < SPAN:
            part = jnp.concatenate([part, jnp.zeros((ROWS, SPAN - part.shape[1]), F32)], axis=1)
        if first is not None:
            part = jnp.where(iota((ROWS, SPAN), 1) < first, 0.0, part)
        return part

    for pair in range(len(blocks) // 2):
        both = jnp.concatenate([value(blocks[2 * pair]), value(blocks[2 * pair + 1])], axis=0)
        left_ref[16 * pair : 16 * pair + 16, :] = both.astype(BF16)


def align_windows(res_ref, dec_ref):
    lane = iota((ROWS, TILE), 1)

    def plain(t):
        main = res_ref[8 * t : 8 * t + 8, 0:TILE]
        if t == 0:
            return main
        return main + res_ref[8 * t - 8 : 8 * t, TILE : 2 * TILE]

    def window(w):
        t = NT * w // TILE
        shift = NT * w - TILE * t
        tiles = [plain(t + u) for u in range(1, 13 if shift else 12)]
        if w == 0:
            first = plain(0)
        else:
            at = 8 * (TILES + w - 1)
            first = res_ref[at : at + 8, 0:TILE]
        tiles = [first] + tiles
        if shift:
            rolled = [pltpu.roll(one, TILE - shift, 1) for one in tiles]
            tiles = [
                jnp.where(lane < TILE - shift, rolled[u], rolled[u + 1]) for u in range(12)
            ]
        return jnp.concatenate(tiles, axis=1)

    for pair in range(WIN // 2):
        both = jnp.concatenate([window(2 * pair), window(2 * pair + 1)], axis=0)
        dec_ref[16 * pair : 16 * pair + 16, :] = both.astype(BF16)


def pack(white, send_ref):
    lane = iota((ROWS, 256), 1)
    segment = lane // GROUP
    wrapped = (lane + 256) // GROUP
    turned = []
    for part in range(2):
        for w in range(WIN):
            spot = part * WIN + w
            piece = white[8 * w : 8 * w + 8, 256 * part : 256 * part + 256]
            turned.append(pltpu.roll(piece, GROUP * spot, 1) if spot else piece)
    for group in range(BINS // GROUP):
        halves = []
        for half in range(2):
            lanes = slice(TILE * half, TILE * half + TILE)
            total = jnp.zeros((ROWS, TILE), F32)
            for spot in range(2 * WIN):
                start = GROUP * (spot + group)
                covers = [
                    at
                    for at in (start, start - 256)
                    if at < TILE * half + TILE and at + GROUP > TILE * half
                ]
                for at in covers:
                    ids = segment if at == start else wrapped
                    total = jnp.where(
                        ids[:, lanes] == spot + group, turned[spot][:, lanes], total
                    )
            halves.append(total)
        dest = jnp.concatenate(halves, axis=1)
        if group:
            dest = pltpu.roll(dest, 256 - GROUP * group, 1)
        both = jnp.concatenate([dest[:, 0:TILE], dest[:, TILE:256]], axis=0)
        z, g = group // 5, group % 5
        send_ref[z, :, TILE * g : TILE * g + TILE] = both.astype(BF16)


def spectra(x_ref, loaded, taps_ref, bins_ref, mask_ref, send_ref, fir_ref, table_ref, left_ref, res_ref, dec_ref):
    build_fir(taps_ref, fir_ref)
    build_table(bins_ref, table_ref)
    loaded.wait()
    build_left(x_ref, left_ref)
    res_ref[...] = jnp.dot(left_ref[...], fir_ref[...], preferred_element_type=F32)
    align_windows(res_ref, dec_ref)
    spectrum = jnp.dot(dec_ref[...], table_ref[...], preferred_element_type=F32)
    power = jnp.sum(spectrum * spectrum, axis=1, keepdims=True) / BINS
    channel = iota((80, 8), 0) % ROWS
    live = jnp.broadcast_to(mask_ref[...].astype(F32), (80, 8))
    live = jnp.sum(jnp.where(channel == iota((80, 8), 1), live, 0.0), axis=1, keepdims=True)
    white = spectrum * (lax.rsqrt(power + 1e-06) * live)
    pack(white, send_ref)


def schedule():
    steps = []

    def begin(h):
        for d in (1, -1, 2):
            steps.append(("near", h, d))
        for v in (1, -1, 2):
            steps.append(("far", h, 0, v))

    def go_on(h):
        for d in (1, -1, 2):
            u = d if d == 2 else -d
            steps.append(("near_wait", h, d))
            for v in (1, -1, 2):
                steps.append(("far", h, u, v))

    def finish(h):
        for u in (0, -1, 1, 2):
            for v in (1, -1, 2):
                steps.append(("far_wait", h, u, v))
            steps.append(("share", h, u))

    steps.append(("take", 0))
    begin(0)
    steps.append(("take", 1))
    begin(1)
    go_on(0)
    go_on(1)
    finish(0)
    finish(1)
    return steps


SCHEDULE = schedule()
COPIES = 2 * sum(step[0] in ("near", "far", "relay", "share") for step in SCHEDULE)


def gather_kernel(
    x_ref, taps_ref, bins_ref, mask_ref, own_ref, all_ref,
    x_here, taps_here, bins_here, mask_here, fir_ref, table_ref, left_ref, res_ref, dec_ref, send_ref, raw,
    in_sem, z_send, z_recv, g_send, g_recv,
):
    z = lax.axis_index("freq")
    b = lax.axis_index("chan")
    x, y, c = b // 8, (b // 2) % 4, b % 2

    def index(xx, yy, cc):
        return (xx % 4 * 4 + yy % 4) * 2 + cc

    sibling = index(x, y, 1 - c)
    peers = [((z + d) % 4, b) for d in (1, 2, 3)]
    peers += [(z, index(x + d, y, c)) for d in (1, 2, 3)]
    peers += [(z, index(x, y + d, c)) for d in (1, 2, 3)]
    peers += [(z, sibling)]
    barrier = pltpu.get_barrier_semaphore()
    for peer in peers:
        pl.semaphore_signal(barrier, inc=1, device_id=peer, device_id_type=MESH)

    small = []
    for at, (src, dst) in enumerate(((taps_ref, taps_here), (bins_ref, bins_here), (mask_ref, mask_here))):
        copy = pltpu.make_async_copy(src, dst, in_sem.at[at])
        copy.start()
        small.append(copy)
    loaded = pltpu.make_async_copy(x_ref, x_here, in_sem.at[3])
    loaded.start()
    for copy in small:
        copy.wait()
    spectra(
        x_here, loaded, taps_here, bins_here, mask_here, send_ref,
        fir_ref, table_ref, left_ref, res_ref, dec_ref,
    )
    pl.semaphore_wait(barrier, len(peers))

    crossing, landed = [], {}
    for d in (2, 1, 3):
        to = (z + d) % 4
        copy = pltpu.make_async_remote_copy(
            src_ref=send_ref.at[to], dst_ref=raw.at[z],
            send_sem=z_send.at[d - 1], recv_sem=z_recv.at[d - 1],
            device_id=(to, b), device_id_type=MESH,
        )
        copy.start()
        crossing.append(copy)
        landed[d] = copy
    raw[z] = send_ref[z]

    started, shares = [], []

    def push(region, target):
        at = len(started)
        copy = pltpu.make_async_remote_copy(
            src_ref=region, dst_ref=region, send_sem=g_send.at[at], recv_sem=g_recv.at[at],
            device_id=(z, target), device_id_type=MESH,
        )
        copy.start()
        started.append(copy)
        return copy

    def place(route, u, v):
        return ((x + u) % 4, (y + v) % 4) if route == 0 else ((x + v) % 4, (y + u) % 4)

    def part(half, route):
        return pl.ds(16 * half, 16), pl.ds(PACK * route, PACK)

    def send(half, route, u, u_to, v_to):
        xx, yy = place(route, u, 0)
        region = all_ref.at[(xx, yy, c) + part(half, route)]
        return push(region, index(*place(route, u_to, v_to), c))

    def share(half, route, u):
        xx, yy = place(route, u, 0)
        if route == 0:
            region = all_ref.at[(xx, slice(None), c) + part(half, route)]
        else:
            region = all_ref.at[(slice(None), yy, c) + part(half, route)]
        shares.append(push(region, sibling))

    near, far = {}, {}

    def unite(half):
        rows = slice(16 * half, 16 * half + 16)
        even = raw[2 * half].astype(F32)
        odd = raw[2 * half + 1].astype(F32)
        low = jnp.concatenate([even[0:8], odd[0:8]], axis=0).astype(BF16)
        high = jnp.concatenate([even[8:16], odd[8:16]], axis=0).astype(BF16)
        for at in range(10):
            source = high if at % 2 else low
            piece = source[:, TILE * (at // 2) : TILE * (at // 2) + TILE]
            lanes = slice(TILE * at, TILE * at + TILE)
            own_ref[rows, lanes] = piece
            all_ref[x, y, c, rows, lanes] = piece

    def arrive(source):
        for d in (1, 2, 3):
            @pl.when((z - source + 4) % 4 == d)
            def _():
                landed[d].wait_recv()

    relayed = {}
    for kind, half, *rest in SCHEDULE:
        if kind == "take":
            arrive(2 * half)
            arrive(2 * half + 1)
            unite(half)
            continue
        for route in (0, 1):
            if kind == "near":
                near[half, route, rest[0]] = send(half, route, 0, rest[0], 0)
            elif kind == "far":
                u, v = rest
                far[half, route, u, v] = send(half, route, u, 0, v)
            elif kind == "near_wait":
                near[half, route, rest[0]].wait_recv()
            elif kind == "far_wait":
                far[(half, route, *rest)].wait_recv()
            elif kind == "relay":
                u, v = rest
                xx, yy = place(route, u, -v)
                region = all_ref.at[(xx, yy, c) + part(half, route)]
                relayed[half, route, u] = push(region, index(*place(route, 0, v), c))
            elif kind == "relay_wait":
                relayed[half, route, rest[0]].wait_recv()
            else:
                share(half, route, rest[0])
    for copy in shares:
        copy.wait_recv()
    for copy in started + crossing:
        copy.wait_send()


def gather(raw_strain, fir_taps, band_bins, live_mask):
    vmem = pl.BlockSpec(memory_space=pltpu.VMEM)
    hbm = pl.BlockSpec(memory_space=pltpu.HBM)
    arrays = (raw_strain, fir_taps.reshape(1, TAPS), band_bins.reshape(1, BINS), live_mask)
    arrays = [pltpu.with_memory_space_constraint(one, pltpu.HBM) for one in arrays]
    return pl.pallas_call(
        gather_kernel,
        out_shape=(
            jax.ShapeDtypeStruct((32, WIDE), BF16),
            jax.ShapeDtypeStruct((4, 4, 2, 32, WIDE), BF16),
        ),
        in_specs=[hbm] * 4,
        out_specs=(vmem, vmem),
        scratch_shapes=[
            pltpu.VMEM((1, ROWS, SAMPLES), BF16),
            pltpu.VMEM((1, TAPS), BF16),
            pltpu.VMEM((1, BINS), I32),
            pltpu.VMEM((1, 8), I32),
            pltpu.VMEM((SPAN, 256), BF16),
            pltpu.VMEM((NTP, 512), BF16),
            pltpu.VMEM((1024, SPAN), BF16),
            pltpu.VMEM((1024, 256), F32),
            pltpu.VMEM((80, NTP), BF16),
            pltpu.VMEM((4, 16, PACK), BF16),
            pltpu.VMEM((4, 16, PACK), BF16),
            pltpu.SemaphoreType.DMA((4,)),
            pltpu.SemaphoreType.DMA((3,)),
            pltpu.SemaphoreType.DMA((3,)),
            pltpu.SemaphoreType.DMA((COPIES,)),
            pltpu.SemaphoreType.DMA((COPIES,)),
        ],
        compiler_params=pltpu.CompilerParams(
            collective_id=0, has_side_effects=True, vmem_limit_bytes=32 * 1024 * 1024
        ),
        name="gather",
    )(*arrays)


SLOTS = 8
STEP = 4


def correlate_kernel(own_ref, all_ref, out_ref, left_ref, slot_ref, sem):
    lane = iota((32, 256), 1)
    copies = []
    for g in range(5):
        lanes = slice(256 * g, 256 * g + 256)
        own = own_ref[:, lanes].astype(F32)
        turned = jnp.where(
            lane < 120,
            pltpu.roll(own, 256 - 120, 1),
            jnp.where(lane < 240, -pltpu.roll(own, 120, 1), 0.0),
        )
        for f in range(GROUP):
            keep = lane % GROUP == f
            both = jnp.concatenate([jnp.where(keep, own, 0.0), jnp.where(keep, turned, 0.0)], axis=0)
            left_ref[64 * f : 64 * f + 64, :] = both.astype(BF16)
        right = all_ref[:, :, lanes].reshape(1024, 256)
        for first in range(0, GROUP, STEP):
            at = len(copies)
            slot = at % SLOTS
            if at >= SLOTS:
                copies[at - SLOTS].wait()
            left = left_ref[64 * first : 64 * (first + STEP), :]
            prod = lax.dot_general(left, right, (((1,), (1,)), ((), ())), preferred_element_type=F32)
            slot_ref[slot] = (prod * (1.0 / WIN)).reshape(STEP, 2, 32, 1024)
            copy = pltpu.make_async_copy(
                slot_ref.at[slot], out_ref.at[pl.ds(GROUP * g + first, STEP)], sem.at[slot]
            )
            copy.start()
            copies.append(copy)
    for copy in copies[-SLOTS:]:
        copy.wait()


def correlate(own, everyone):
    vmem = pl.BlockSpec(memory_space=pltpu.VMEM)
    return pl.pallas_call(
        correlate_kernel,
        out_shape=jax.ShapeDtypeStruct((60, 2, 32, 1024), F32),
        in_specs=[vmem, vmem],
        out_specs=pl.BlockSpec(memory_space=pltpu.HBM),
        scratch_shapes=[
            pltpu.VMEM((64 * GROUP, 256), BF16),
            pltpu.VMEM((SLOTS, STEP, 2, 32, 1024), F32),
            pltpu.SemaphoreType.DMA((SLOTS,)),
        ],
        compiler_params=pltpu.CompilerParams(vmem_limit_bytes=32 * 1024 * 1024),
        name="correlate",
    )(own, everyone)


def shards(raw_strain, fir_taps, band_bins, live_mask):
    own, everyone = gather(raw_strain, fir_taps, band_bins, live_mask)
    return correlate(own, everyone.reshape(32, 32, WIDE))


def solution(mesh):
    in_specs = (P("chan", "freq", None), P(), P(), P("chan", "freq"))
    out_specs = P("freq", None, "chan", None)
    return jax.shard_map(shards, mesh=mesh, in_specs=in_specs, out_specs=out_specs, check_vma=False)
```

```python
import functools
import math

import jax
import jax.numpy as jnp
from jax import lax
from jax.experimental import pallas as pl
from jax.experimental.pallas import tpu as pltpu
from jax.sharding import PartitionSpec as P

WIN = 10
DECIM = 10
NT = 1500
TAPS = 20
BINS = 240
ROWS = 8
TILE = 128
SPAN = TILE * DECIM
SAMPLES = WIN * NT * DECIM
TILES = -(-SAMPLES // SPAN)
NTP = 12 * TILE
GROUP = 12
PACK = 5 * TILE
WIDE = 5 * 256
F32 = jnp.float32
BF16 = jnp.bfloat16
I32 = jnp.int32
MESH = pl.DeviceIdType.MESH


def iota(shape, axis):
    return lax.broadcasted_iota(I32, shape, axis)


def build_fir(taps_ref, fir_ref):
    row = iota((80, TAPS), 0)
    phase = row % DECIM
    tap = iota((80, TAPS), 1)
    taps = jnp.broadcast_to(taps_ref[...].astype(F32), (80, TAPS))
    near = jnp.sum(jnp.where(tap == 9 - phase, taps, 0.0), axis=1, keepdims=True)
    far = jnp.sum(jnp.where(tap == 19 - phase, taps, 0.0), axis=1, keepdims=True)
    near = jnp.broadcast_to(near, (80, 256))
    far = jnp.broadcast_to(far, (80, 256))
    gap = iota((80, 256), 1) - iota((80, 256), 0) // DECIM
    for step in range(SPAN // 80):
        block = jnp.where(gap == 8 * step, near, jnp.where(gap == 8 * step + 1, far, 0.0))
        fir_ref[80 * step : 80 * step + 80, :] = block.astype(BF16)


def build_table(bins_ref, table_ref):
    bins = bins_ref[...].astype(F32)
    bins = jnp.concatenate([bins, jnp.zeros((1, 16), F32)], axis=1)
    row = iota((40, 256), 0)
    times = jnp.where(row < 8, row, jnp.where(row < 24, 8 * (row - 8), 128 * (row - 24)))
    product = times.astype(F32) * bins
    turns = jnp.floor(product * (1.0 / NT))
    left = product - turns * NT
    left = jnp.where(left < 0, left + NT, left)
    left = jnp.where(left >= NT, left - NT, left)
    angle = left * F32(2.0 * math.pi / NT)
    re = jnp.cos(angle)
    im = -jnp.sin(angle)
    kept = iota((40, 256), 1) < BINS
    re = jnp.where(kept, re, 0.0)
    im = jnp.where(kept, im, 0.0)
    base_re, base_im = [], []
    for b in range(16):
        tr, ti = re[8 + b : 9 + b], im[8 + b : 9 + b]
        base_re.append(re[0:8] * tr - im[0:8] * ti)
        base_im.append(re[0:8] * ti + im[0:8] * tr)
    base_re = jnp.concatenate(base_re, axis=0)
    base_im = jnp.concatenate(base_im, axis=0)
    for a in range(12):
        tr, ti = re[24 + a : 25 + a], im[24 + a : 25 + a]
        block_re = base_re * tr - base_im * ti
        block_im = base_re * ti + base_im * tr
        if a == 11:
            inside = iota((TILE, 256), 0) < NT - 11 * TILE
            block_re = jnp.where(inside, block_re, 0.0)
            block_im = jnp.where(inside, block_im, 0.0)
        table_ref[TILE * a : TILE * a + TILE, 0:256] = block_re.astype(BF16)
        table_ref[TILE * a : TILE * a + TILE, 256:512] = block_im.astype(BF16)


def build_left(x_ref, left_ref):
    def tile(t):
        return x_ref[0, :, SPAN * t : min(SPAN * t + SPAN, SAMPLES)].astype(F32)

    blocks = [(t, None) for t in range(TILES)]
    for w in range(1, WIN):
        t = NT * w // TILE
        blocks.append((t, NT * DECIM * w - SPAN * t))
    blocks.append((None, None))

    def value(block):
        t, first = block
        if t is None:
            return jnp.zeros((ROWS, SPAN), F32)
        part = tile(t)
        if part.shape[1] < SPAN:
            part = jnp.concatenate([part, jnp.zeros((ROWS, SPAN - part.shape[1]), F32)], axis=1)
        if first is not None:
            part = jnp.where(iota((ROWS, SPAN), 1) < first, 0.0, part)
        return part

    for pair in range(len(blocks) // 2):
        both = jnp.concatenate([value(blocks[2 * pair]), value(blocks[2 * pair + 1])], axis=0)
        left_ref[16 * pair : 16 * pair + 16, :] = both.astype(BF16)


def align_windows(res_ref, dec_ref):
    lane = iota((ROWS, TILE), 1)

    def plain(t):
        main = res_ref[8 * t : 8 * t + 8, 0:TILE]
        if t == 0:
            return main
        return main + res_ref[8 * t - 8 : 8 * t, TILE : 2 * TILE]

    def window(w):
        t = NT * w // TILE
        shift = NT * w - TILE * t
        tiles = [plain(t + u) for u in range(1, 13 if shift else 12)]
        if w == 0:
            first = plain(0)
        else:
            at = 8 * (TILES + w - 1)
            first = res_ref[at : at + 8, 0:TILE]
        tiles = [first] + tiles
        if shift:
            rolled = [pltpu.roll(one, TILE - shift, 1) for one in tiles]
            tiles = [
                jnp.where(lane < TILE - shift, rolled[u], rolled[u + 1]) for u in range(12)
            ]
        return jnp.concatenate(tiles, axis=1)

    for pair in range(WIN // 2):
        both = jnp.concatenate([window(2 * pair), window(2 * pair + 1)], axis=0)
        dec_ref[16 * pair : 16 * pair + 16, :] = both.astype(BF16)


def pack(white, send_ref):
    lane = iota((ROWS, 256), 1)
    segment = lane // GROUP
    wrapped = (lane + 256) // GROUP
    turned = []
    for part in range(2):
        for w in range(WIN):
            spot = part * WIN + w
            piece = white[8 * w : 8 * w + 8, 256 * part : 256 * part + 256]
            turned.append(pltpu.roll(piece, GROUP * spot, 1) if spot else piece)
    for group in range(BINS // GROUP):
        halves = []
        for half in range(2):
            lanes = slice(TILE * half, TILE * half + TILE)
            total = jnp.zeros((ROWS, TILE), F32)
            for spot in range(2 * WIN):
                start = GROUP * (spot + group)
                covers = [
                    at
                    for at in (start, start - 256)
                    if at < TILE * half + TILE and at + GROUP > TILE * half
                ]
                for at in covers:
                    ids = segment if at == start else wrapped
                    total = jnp.where(
                        ids[:, lanes] == spot + group, turned[spot][:, lanes], total
                    )
            halves.append(total)
        dest = jnp.concatenate(halves, axis=1)
        if group:
            dest = pltpu.roll(dest, 256 - GROUP * group, 1)
        both = jnp.concatenate([dest[:, 0:TILE], dest[:, TILE:256]], axis=0)
        z, g = group // 5, group % 5
        send_ref[z, :, TILE * g : TILE * g + TILE] = both.astype(BF16)


def spectra(x_ref, loaded, taps_ref, bins_ref, mask_ref, send_ref, fir_ref, table_ref, left_ref, res_ref, dec_ref):
    build_fir(taps_ref, fir_ref)
    build_table(bins_ref, table_ref)
    loaded.wait()
    build_left(x_ref, left_ref)
    res_ref[...] = jnp.dot(left_ref[...], fir_ref[...], preferred_element_type=F32)
    align_windows(res_ref, dec_ref)
    spectrum = jnp.dot(dec_ref[...], table_ref[...], preferred_element_type=F32)
    power = jnp.sum(spectrum * spectrum, axis=1, keepdims=True) / BINS
    channel = iota((80, 8), 0) % ROWS
    live = jnp.broadcast_to(mask_ref[...].astype(F32), (80, 8))
    live = jnp.sum(jnp.where(channel == iota((80, 8), 1), live, 0.0), axis=1, keepdims=True)
    white = spectrum * (lax.rsqrt(power + 1e-06) * live)
    pack(white, send_ref)


def schedule():
    steps = []

    def begin(h):
        for d in (1, -1, 2):
            steps.append(("near", h, d))
        for v in (1, -1, 2):
            steps.append(("far", h, 0, v))

    def go_on(h):
        for d in (1, -1, 2):
            u = d if d == 2 else -d
            steps.append(("near_wait", h, d))
            for v in (1, -1, 2):
                steps.append(("far", h, u, v))

    def finish(h):
        for u in (0, -1, 1, 2):
            steps.append(("far_wait", h, u))
            steps.append(("share", h, u))

    steps.append(("take", 0))
    begin(0)
    steps.append(("take", 1))
    begin(1)
    go_on(0)
    go_on(1)
    finish(0)
    steps.append(("drain", 0))
    finish(1)
    return steps


SCHEDULE = schedule()


def gather_kernel(
    x_ref, taps_ref, bins_ref, mask_ref, own_ref, all_ref,
    x_here, taps_here, bins_here, mask_here, fir_ref, table_ref, left_ref, res_ref, dec_ref, send_ref, raw,
    in_sem, z_send, z_recv, sent_sem, near_recv, far_recv, share_sem,
):
    z = lax.axis_index("freq")
    b = lax.axis_index("chan")
    x, y, c = b // 8, (b // 2) % 4, b % 2

    def index(xx, yy, cc):
        return (xx % 4 * 4 + yy % 4) * 2 + cc

    sibling = index(x, y, 1 - c)
    peers = [((z + d) % 4, b) for d in (1, 2, 3)]
    peers += [(z, index(x + d, y, c)) for d in (1, 2, 3)]
    peers += [(z, index(x, y + d, c)) for d in (1, 2, 3)]
    peers += [(z, sibling)]
    barrier = pltpu.get_barrier_semaphore()
    for peer in peers:
        pl.semaphore_signal(barrier, inc=1, device_id=peer, device_id_type=MESH)

    small = []
    for at, (src, dst) in enumerate(((taps_ref, taps_here), (bins_ref, bins_here), (mask_ref, mask_here))):
        copy = pltpu.make_async_copy(src, dst, in_sem.at[at])
        copy.start()
        small.append(copy)
    loaded = pltpu.make_async_copy(x_ref, x_here, in_sem.at[3])
    loaded.start()
    for copy in small:
        copy.wait()
    spectra(
        x_here, loaded, taps_here, bins_here, mask_here, send_ref,
        fir_ref, table_ref, left_ref, res_ref, dec_ref,
    )
    pl.semaphore_wait(barrier, len(peers))

    crossing, landed = [], {}
    for d in (2, 1, 3):
        to = (z + d) % 4
        copy = pltpu.make_async_remote_copy(
            src_ref=send_ref.at[to], dst_ref=raw.at[z],
            send_sem=z_send.at[d - 1], recv_sem=z_recv.at[d - 1],
            device_id=(to, b), device_id_type=MESH,
        )
        copy.start()
        crossing.append(copy)
        landed[d] = copy
    raw[z] = send_ref[z]

    def push(region, target, sent, landed):
        pltpu.make_async_remote_copy(
            src_ref=region, dst_ref=region, send_sem=sent, recv_sem=landed,
            device_id=(z, target), device_id_type=MESH,
        ).start()

    def wait_for(region, sem):
        pltpu.make_async_copy(region, region, sem).wait()

    xs = {d: lax.rem(x + d % 4, 4) for d in (0, 1, -1, 2)}
    ys = {d: lax.rem(y + d % 4, 4) for d in (0, 1, -1, 2)}
    along_x = {d: (xs[d] * 4 + y) * 2 + c for d in (1, -1, 2)}
    along_y = {d: (x * 4 + ys[d]) * 2 + c for d in (1, -1, 2)}

    def part(half, route):
        return pl.ds(16 * half, 16), pl.ds(PACK * route, PACK)

    def block(half, route, u):
        xx, yy = (xs[u], y) if route == 0 else (x, ys[u])
        return all_ref.at[(xx, yy, c) + part(half, route)]

    def share(half, route, u):
        if route == 0:
            region = all_ref.at[(xs[u], slice(None), c) + part(half, route)]
        else:
            region = all_ref.at[(slice(None), ys[u], c) + part(half, route)]
        push(region, sibling, sent_sem.at[2], share_sem.at[0])

    def near_sem(half, route, d):
        return near_recv.at[6 * half + 3 * route + (1, -1, 2).index(d)]

    def far_sem(half, route, u):
        return far_recv.at[8 * half + 4 * route + u % 4]

    def unite(half):
        rows = slice(16 * half, 16 * half + 16)
        even = raw[2 * half].astype(F32)
        odd = raw[2 * half + 1].astype(F32)
        low = jnp.concatenate([even[0:8], odd[0:8]], axis=0).astype(BF16)
        high = jnp.concatenate([even[8:16], odd[8:16]], axis=0).astype(BF16)
        for at in range(10):
            source = high if at % 2 else low
            piece = source[:, TILE * (at // 2) : TILE * (at // 2) + TILE]
            lanes = slice(TILE * at, TILE * at + TILE)
            own_ref[rows, lanes] = piece
            all_ref[x, y, c, rows, lanes] = piece

    def arrive(source):
        for d in (1, 2, 3):
            @pl.when((z - source + 4) % 4 == d)
            def _():
                landed[d].wait_recv()

    for kind, half, *rest in SCHEDULE:
        if kind == "take":
            arrive(2 * half)
            arrive(2 * half + 1)
            unite(half)
            continue
        if kind == "drain":
            wait_for(all_ref.at[0, pl.ds(0, 3), 0], sent_sem.at[0])
            wait_for(all_ref.at[pl.ds(0, 3), :, 0], sent_sem.at[1])
            for copy in crossing:
                copy.wait_send()
            continue
        for route in (0, 1):
            if kind == "near":
                to = (along_x if route == 0 else along_y)[rest[0]]
                push(block(half, route, 0), to, sent_sem.at[0], near_sem(half, route, rest[0]))
            elif kind == "near_wait":
                wait_for(block(half, route, 0), near_sem(half, route, rest[0]))
            elif kind == "far":
                u, v = rest
                to = (along_y if route == 0 else along_x)[v]
                push(block(half, route, u), to, sent_sem.at[1], far_sem(half, route, u))
            elif kind == "far_wait":
                three = all_ref.at[(pl.ds(0, 3), 0, 0) + part(half, route)]
                wait_for(three, far_sem(half, route, rest[0]))
            else:
                share(half, route, rest[0])
    wait_for(all_ref.at[:, :, 0], share_sem.at[0])
    wait_for(all_ref.at[:, :, 0], sent_sem.at[2])


def gather(raw_strain, fir_taps, band_bins, live_mask):
    vmem = pl.BlockSpec(memory_space=pltpu.VMEM)
    hbm = pl.BlockSpec(memory_space=pltpu.HBM)
    arrays = (raw_strain, fir_taps.reshape(1, TAPS), band_bins.reshape(1, BINS), live_mask)
    arrays = [pltpu.with_memory_space_constraint(one, pltpu.HBM) for one in arrays]
    return pl.pallas_call(
        gather_kernel,
        out_shape=(
            jax.ShapeDtypeStruct((32, WIDE), BF16),
            jax.ShapeDtypeStruct((4, 4, 2, 32, WIDE), BF16),
        ),
        in_specs=[hbm] * 4,
        out_specs=(vmem, vmem),
        scratch_shapes=[
            pltpu.VMEM((1, ROWS, SAMPLES), BF16),
            pltpu.VMEM((1, TAPS), BF16),
            pltpu.VMEM((1, BINS), I32),
            pltpu.VMEM((1, 8), I32),
            pltpu.VMEM((SPAN, 256), BF16),
            pltpu.VMEM((NTP, 512), BF16),
            pltpu.VMEM((1024, SPAN), BF16),
            pltpu.VMEM((1024, 256), F32),
            pltpu.VMEM((80, NTP), BF16),
            pltpu.VMEM((4, 16, PACK), BF16),
            pltpu.VMEM((4, 16, PACK), BF16),
            pltpu.SemaphoreType.DMA((4,)),
            pltpu.SemaphoreType.DMA((3,)),
            pltpu.SemaphoreType.DMA((3,)),
            pltpu.SemaphoreType.DMA((3,)),
            pltpu.SemaphoreType.DMA((12,)),
            pltpu.SemaphoreType.DMA((16,)),
            pltpu.SemaphoreType.DMA((1,)),
        ],
        compiler_params=pltpu.CompilerParams(
            collective_id=0, has_side_effects=True, vmem_limit_bytes=32 * 1024 * 1024
        ),
        name="gather",
    )(*arrays)


SLOTS = 8
STEP = 4


def correlate_kernel(own_ref, all_ref, out_ref, left_ref, slot_ref, sem):
    lane = iota((32, 256), 1)
    copies = []
    for g in range(5):
        lanes = slice(256 * g, 256 * g + 256)
        own = own_ref[:, lanes].astype(F32)
        turned = jnp.where(
            lane < 120,
            pltpu.roll(own, 256 - 120, 1),
            jnp.where(lane < 240, -pltpu.roll(own, 120, 1), 0.0),
        )
        for f in range(GROUP):
            keep = lane % GROUP == f
            both = jnp.concatenate([jnp.where(keep, own, 0.0), jnp.where(keep, turned, 0.0)], axis=0)
            left_ref[64 * f : 64 * f + 64, :] = both.astype(BF16)
        right = all_ref[:, :, lanes].reshape(1024, 256)
        for first in range(0, GROUP, STEP):
            at = len(copies)
            slot = at % SLOTS
            if at >= SLOTS:
                copies[at - SLOTS].wait()
            left = left_ref[64 * first : 64 * (first + STEP), :]
            prod = lax.dot_general(left, right, (((1,), (1,)), ((), ())), preferred_element_type=F32)
            slot_ref[slot] = (prod * (1.0 / WIN)).reshape(STEP, 2, 32, 1024)
            copy = pltpu.make_async_copy(
                slot_ref.at[slot], out_ref.at[pl.ds(GROUP * g + first, STEP)], sem.at[slot]
            )
            copy.start()
            copies.append(copy)
    for copy in copies[-SLOTS:]:
        copy.wait()


def correlate(own, everyone):
    vmem = pl.BlockSpec(memory_space=pltpu.VMEM)
    return pl.pallas_call(
        correlate_kernel,
        out_shape=jax.ShapeDtypeStruct((60, 2, 32, 1024), F32),
        in_specs=[vmem, vmem],
        out_specs=pl.BlockSpec(memory_space=pltpu.HBM),
        scratch_shapes=[
            pltpu.VMEM((64 * GROUP, 256), BF16),
            pltpu.VMEM((SLOTS, STEP, 2, 32, 1024), F32),
            pltpu.SemaphoreType.DMA((SLOTS,)),
        ],
        compiler_params=pltpu.CompilerParams(vmem_limit_bytes=32 * 1024 * 1024),
        name="correlate",
    )(own, everyone)


def shards(raw_strain, fir_taps, band_bins, live_mask):
    own, everyone = gather(raw_strain, fir_taps, band_bins, live_mask)
    return correlate(own, everyone.reshape(32, 32, WIDE))


def solution(mesh):
    in_specs = (P("chan", "freq", None), P(), P(), P("chan", "freq"))
    out_specs = P("freq", None, "chan", None)
    return jax.shard_map(shards, mesh=mesh, in_specs=in_specs, out_specs=out_specs, check_vma=False)
```

```python
import functools
import math

import jax
import jax.numpy as jnp
from jax import lax
from jax.experimental import pallas as pl
from jax.experimental.pallas import tpu as pltpu
from jax.sharding import PartitionSpec as P

WIN = 10
DECIM = 10
NT = 1500
TAPS = 20
BINS = 240
ROWS = 8
TILE = 128
SPAN = TILE * DECIM
SAMPLES = WIN * NT * DECIM
TILES = -(-SAMPLES // SPAN)
NTP = 12 * TILE
GROUP = 12
PACK = 5 * TILE
WIDE = 5 * 256
F32 = jnp.float32
BF16 = jnp.bfloat16
I32 = jnp.int32
MESH = pl.DeviceIdType.MESH


def iota(shape, axis):
    return lax.broadcasted_iota(I32, shape, axis)


def build_fir(taps_ref, fir_ref):
    row = iota((80, TAPS), 0)
    phase = row % DECIM
    tap = iota((80, TAPS), 1)
    taps = jnp.broadcast_to(taps_ref[...].astype(F32), (80, TAPS))
    near = jnp.sum(jnp.where(tap == 9 - phase, taps, 0.0), axis=1, keepdims=True)
    far = jnp.sum(jnp.where(tap == 19 - phase, taps, 0.0), axis=1, keepdims=True)
    near = jnp.broadcast_to(near, (80, 256))
    far = jnp.broadcast_to(far, (80, 256))
    gap = iota((80, 256), 1) - iota((80, 256), 0) // DECIM
    for step in range(SPAN // 80):
        block = jnp.where(gap == 8 * step, near, jnp.where(gap == 8 * step + 1, far, 0.0))
        fir_ref[80 * step : 80 * step + 80, :] = block.astype(BF16)


def build_table(bins_ref, table_ref):
    bins = bins_ref[...].astype(F32)
    bins = jnp.concatenate([bins, jnp.zeros((1, 16), F32)], axis=1)
    row = iota((40, 256), 0)
    times = jnp.where(row < 8, row, jnp.where(row < 24, 8 * (row - 8), 128 * (row - 24)))
    product = times.astype(F32) * bins
    turns = jnp.floor(product * (1.0 / NT))
    left = product - turns * NT
    left = jnp.where(left < 0, left + NT, left)
    left = jnp.where(left >= NT, left - NT, left)
    angle = left * F32(2.0 * math.pi / NT)
    re = jnp.cos(angle)
    im = -jnp.sin(angle)
    kept = iota((40, 256), 1) < BINS
    re = jnp.where(kept, re, 0.0)
    im = jnp.where(kept, im, 0.0)
    base_re, base_im = [], []
    for b in range(16):
        tr, ti = re[8 + b : 9 + b], im[8 + b : 9 + b]
        base_re.append(re[0:8] * tr - im[0:8] * ti)
        base_im.append(re[0:8] * ti + im[0:8] * tr)
    base_re = jnp.concatenate(base_re, axis=0)
    base_im = jnp.concatenate(base_im, axis=0)
    for a in range(12):
        tr, ti = re[24 + a : 25 + a], im[24 + a : 25 + a]
        block_re = base_re * tr - base_im * ti
        block_im = base_re * ti + base_im * tr
        if a == 11:
            inside = iota((TILE, 256), 0) < NT - 11 * TILE
            block_re = jnp.where(inside, block_re, 0.0)
            block_im = jnp.where(inside, block_im, 0.0)
        table_ref[TILE * a : TILE * a + TILE, 0:256] = block_re.astype(BF16)
        table_ref[TILE * a : TILE * a + TILE, 256:512] = block_im.astype(BF16)


def build_left(x_ref, left_ref):
    def tile(t):
        return x_ref[0, :, SPAN * t : min(SPAN * t + SPAN, SAMPLES)].astype(F32)

    blocks = [(t, None) for t in range(TILES)]
    for w in range(1, WIN):
        t = NT * w // TILE
        blocks.append((t, NT * DECIM * w - SPAN * t))
    blocks.append((None, None))

    def value(block):
        t, first = block
        if t is None:
            return jnp.zeros((ROWS, SPAN), F32)
        part = tile(t)
        if part.shape[1] < SPAN:
            part = jnp.concatenate([part, jnp.zeros((ROWS, SPAN - part.shape[1]), F32)], axis=1)
        if first is not None:
            part = jnp.where(iota((ROWS, SPAN), 1) < first, 0.0, part)
        return part

    for pair in range(len(blocks) // 2):
        both = jnp.concatenate([value(blocks[2 * pair]), value(blocks[2 * pair + 1])], axis=0)
        left_ref[16 * pair : 16 * pair + 16, :] = both.astype(BF16)


def align_windows(res_ref, dec_ref):
    lane = iota((ROWS, TILE), 1)

    def plain(t):
        main = res_ref[8 * t : 8 * t + 8, 0:TILE]
        if t == 0:
            return main
        return main + res_ref[8 * t - 8 : 8 * t, TILE : 2 * TILE]

    def window(w):
        t = NT * w // TILE
        shift = NT * w - TILE * t
        tiles = [plain(t + u) for u in range(1, 13 if shift else 12)]
        if w == 0:
            first = plain(0)
        else:
            at = 8 * (TILES + w - 1)
            first = res_ref[at : at + 8, 0:TILE]
        tiles = [first] + tiles
        if shift:
            rolled = [pltpu.roll(one, TILE - shift, 1) for one in tiles]
            tiles = [
                jnp.where(lane < TILE - shift, rolled[u], rolled[u + 1]) for u in range(12)
            ]
        return jnp.concatenate(tiles, axis=1)

    for pair in range(WIN // 2):
        both = jnp.concatenate([window(2 * pair), window(2 * pair + 1)], axis=0)
        dec_ref[16 * pair : 16 * pair + 16, :] = both.astype(BF16)


def pack(white, send_ref):
    lane = iota((ROWS, 256), 1)
    segment = lane // GROUP
    wrapped = (lane + 256) // GROUP
    turned = []
    for part in range(2):
        for w in range(WIN):
            spot = part * WIN + w
            piece = white[8 * w : 8 * w + 8, 256 * part : 256 * part + 256]
            turned.append(pltpu.roll(piece, GROUP * spot, 1) if spot else piece)
    for group in range(BINS // GROUP):
        halves = []
        for half in range(2):
            lanes = slice(TILE * half, TILE * half + TILE)
            total = jnp.zeros((ROWS, TILE), F32)
            for spot in range(2 * WIN):
                start = GROUP * (spot + group)
                covers = [
                    at
                    for at in (start, start - 256)
                    if at < TILE * half + TILE and at + GROUP > TILE * half
                ]
                for at in covers:
                    ids = segment if at == start else wrapped
                    total = jnp.where(
                        ids[:, lanes] == spot + group, turned[spot][:, lanes], total
                    )
            halves.append(total)
        dest = jnp.concatenate(halves, axis=1)
        if group:
            dest = pltpu.roll(dest, 256 - GROUP * group, 1)
        both = jnp.concatenate([dest[:, 0:TILE], dest[:, TILE:256]], axis=0)
        z, g = group // 5, group % 5
        send_ref[z, :, TILE * g : TILE * g + TILE] = both.astype(BF16)


def spectra(x_ref, loaded, taps_ref, bins_ref, mask_ref, send_ref, fir_ref, table_ref, left_ref, res_ref, dec_ref):
    build_fir(taps_ref, fir_ref)
    build_table(bins_ref, table_ref)
    loaded.wait()
    build_left(x_ref, left_ref)
    res_ref[...] = jnp.dot(left_ref[...], fir_ref[...], preferred_element_type=F32)
    align_windows(res_ref, dec_ref)
    spectrum = jnp.dot(dec_ref[...], table_ref[...], preferred_element_type=F32)
    power = jnp.sum(spectrum * spectrum, axis=1, keepdims=True) / BINS
    channel = iota((80, 8), 0) % ROWS
    live = jnp.broadcast_to(mask_ref[...].astype(F32), (80, 8))
    live = jnp.sum(jnp.where(channel == iota((80, 8), 1), live, 0.0), axis=1, keepdims=True)
    white = spectrum * (lax.rsqrt(power + 1e-06) * live)
    pack(white, send_ref)


def schedule():
    steps = []

    def begin(h):
        for d in (1, -1, 2):
            steps.append(("near", h, d))
        for v in (1, -1, 2):
            steps.append(("far", h, 0, v))

    def go_on(h):
        for d in (1, -1, 2):
            u = d if d == 2 else -d
            steps.append(("near_wait", h, d))
            for v in (1, -1, 2):
                steps.append(("far", h, u, v))

    def finish(h):
        for u in (0, -1, 1, 2):
            steps.append(("far_wait", h, u))
            steps.append(("share", h, u))

    steps.append(("take", 0))
    begin(0)
    steps.append(("take", 1))
    begin(1)
    go_on(0)
    go_on(1)
    finish(0)
    steps.append(("drain", 0))
    finish(1)
    return steps


SCHEDULE = schedule()


def gather_kernel(
    x_ref, taps_ref, bins_ref, mask_ref, own_ref, all_ref,
    x_here, taps_here, bins_here, mask_here, fir_ref, table_ref, left_ref, res_ref, dec_ref, send_ref, raw,
    in_sem, z_send, z_recv, sent_sem, near_recv, far_recv, share_sem,
):
    z = lax.axis_index("freq")
    b = lax.axis_index("chan")
    x, y, c = b // 8, (b // 2) % 4, b % 2

    def index(xx, yy, cc):
        return (xx % 4 * 4 + yy % 4) * 2 + cc

    sibling = index(x, y, 1 - c)
    peers = [((z + d) % 4, b) for d in (1, 2, 3)]
    peers += [(z, index(x + d, y, c)) for d in (1, 2, 3)]
    peers += [(z, index(x, y + d, c)) for d in (1, 2, 3)]
    peers += [(z, sibling)]
    barrier = pltpu.get_barrier_semaphore()
    for peer in peers:
        pl.semaphore_signal(barrier, inc=1, device_id=peer, device_id_type=MESH)

    small = []
    for at, (src, dst) in enumerate(((taps_ref, taps_here), (bins_ref, bins_here), (mask_ref, mask_here))):
        copy = pltpu.make_async_copy(src, dst, in_sem.at[at])
        copy.start()
        small.append(copy)
    loaded = pltpu.make_async_copy(x_ref, x_here, in_sem.at[3])
    loaded.start()
    for copy in small:
        copy.wait()
    spectra(
        x_here, loaded, taps_here, bins_here, mask_here, send_ref,
        fir_ref, table_ref, left_ref, res_ref, dec_ref,
    )
    pl.semaphore_wait(barrier, len(peers))

    crossing, landed = [], {}
    for d in (2, 1, 3):
        to = (z + d) % 4
        copy = pltpu.make_async_remote_copy(
            src_ref=send_ref.at[to], dst_ref=raw.at[z],
            send_sem=z_send.at[d - 1], recv_sem=z_recv.at[d - 1],
            device_id=(to, b), device_id_type=MESH,
        )
        copy.start()
        crossing.append(copy)
        landed[d] = copy
    raw[z] = send_ref[z]

    def push(region, target, sent, landed):
        pltpu.make_async_remote_copy(
            src_ref=region, dst_ref=region, send_sem=sent, recv_sem=landed,
            device_id=(z, target), device_id_type=MESH,
        ).start()

    def wait_for(region, sem):
        pltpu.make_async_copy(region, region, sem).wait()

    xs = {d: lax.rem(x + d % 4, 4) for d in (0, 1, -1, 2)}
    ys = {d: lax.rem(y + d % 4, 4) for d in (0, 1, -1, 2)}
    along_x = {d: (xs[d] * 4 + y) * 2 + c for d in (1, -1, 2)}
    along_y = {d: (x * 4 + ys[d]) * 2 + c for d in (1, -1, 2)}

    def part(half, route):
        return pl.ds(16 * half, 16), pl.ds(PACK * route, PACK)

    def block(half, route, u):
        xx, yy = (xs[u], y) if route == 0 else (x, ys[u])
        return all_ref.at[(xx, yy, c) + part(half, route)]

    def share(half, route, u):
        if route == 0:
            region = all_ref.at[(xs[u], slice(None), c) + part(half, route)]
        else:
            region = all_ref.at[(slice(None), ys[u], c) + part(half, route)]
        push(region, sibling, sent_sem.at[2], share_sem.at[0])

    def near_sem(half, route, d):
        return near_recv.at[6 * half + 3 * route + (1, -1, 2).index(d)]

    def far_sem(half, route, u):
        return far_recv.at[8 * half + 4 * route + u % 4]

    def unite(half):
        rows = slice(16 * half, 16 * half + 16)
        even = raw[2 * half].astype(F32)
        odd = raw[2 * half + 1].astype(F32)
        low = jnp.concatenate([even[0:8], odd[0:8]], axis=0).astype(BF16)
        high = jnp.concatenate([even[8:16], odd[8:16]], axis=0).astype(BF16)
        for at in range(10):
            source = high if at % 2 else low
            piece = source[:, TILE * (at // 2) : TILE * (at // 2) + TILE]
            lanes = slice(TILE * at, TILE * at + TILE)
            own_ref[rows, lanes] = piece
            all_ref[x, y, c, rows, lanes] = piece

    def arrive(source):
        for d in (1, 2, 3):
            @pl.when((z - source + 4) % 4 == d)
            def _():
                landed[d].wait_recv()

    for kind, half, *rest in SCHEDULE:
        if kind == "take":
            arrive(2 * half)
            arrive(2 * half + 1)
            unite(half)
            continue
        if kind == "drain":
            wait_for(all_ref.at[0, pl.ds(0, 3), 0], sent_sem.at[0])
            wait_for(all_ref.at[pl.ds(0, 3), :, 0], sent_sem.at[1])
            for copy in crossing:
                copy.wait_send()
            continue
        for route in (0, 1):
            if kind == "near":
                to = (along_x if route == 0 else along_y)[rest[0]]
                push(block(half, route, 0), to, sent_sem.at[0], near_sem(half, route, rest[0]))
            elif kind == "near_wait":
                wait_for(block(half, route, 0), near_sem(half, route, rest[0]))
            elif kind == "far":
                u, v = rest
                to = (along_y if route == 0 else along_x)[v]
                push(block(half, route, u), to, sent_sem.at[1], far_sem(half, route, u))
            elif kind == "far_wait":
                three = all_ref.at[(pl.ds(0, 3), 0, 0) + part(half, route)]
                wait_for(three, far_sem(half, route, rest[0]))
            else:
                share(half, route, rest[0])
    wait_for(all_ref.at[:, :, 0], share_sem.at[0])
    wait_for(all_ref.at[:, :, 0], sent_sem.at[2])


def gather(raw_strain, fir_taps, band_bins, live_mask):
    vmem = pl.BlockSpec(memory_space=pltpu.VMEM)
    hbm = pl.BlockSpec(memory_space=pltpu.HBM)
    arrays = (raw_strain, fir_taps.reshape(1, TAPS), band_bins.reshape(1, BINS), live_mask)
    arrays = [pltpu.with_memory_space_constraint(one, pltpu.HBM) for one in arrays]
    return pl.pallas_call(
        gather_kernel,
        out_shape=(
            jax.ShapeDtypeStruct((32, WIDE), BF16),
            jax.ShapeDtypeStruct((4, 4, 2, 32, WIDE), BF16),
        ),
        in_specs=[hbm] * 4,
        out_specs=(vmem, vmem),
        scratch_shapes=[
            pltpu.VMEM((1, ROWS, SAMPLES), BF16),
            pltpu.VMEM((1, TAPS), BF16),
            pltpu.VMEM((1, BINS), I32),
            pltpu.VMEM((1, 8), I32),
            pltpu.VMEM((SPAN, 256), BF16),
            pltpu.VMEM((NTP, 512), BF16),
            pltpu.VMEM((1024, SPAN), BF16),
            pltpu.VMEM((1024, 256), F32),
            pltpu.VMEM((80, NTP), BF16),
            pltpu.VMEM((4, 16, PACK), BF16),
            pltpu.VMEM((4, 16, PACK), BF16),
            pltpu.SemaphoreType.DMA((4,)),
            pltpu.SemaphoreType.DMA((3,)),
            pltpu.SemaphoreType.DMA((3,)),
            pltpu.SemaphoreType.DMA((3,)),
            pltpu.SemaphoreType.DMA((12,)),
            pltpu.SemaphoreType.DMA((16,)),
            pltpu.SemaphoreType.DMA((1,)),
        ],
        compiler_params=pltpu.CompilerParams(
            collective_id=0, has_side_effects=True, vmem_limit_bytes=32 * 1024 * 1024
        ),
        name="gather",
    )(*arrays)


SLOTS = 8
STEP = 4


def correlate_kernel(own_ref, all_ref, out_ref, left_ref, slot_ref, sem):
    lane = iota((32, 256), 1)
    copies = []
    for g in range(5):
        lanes = slice(256 * g, 256 * g + 256)
        own = own_ref[:, lanes].astype(F32)
        turned = jnp.where(
            lane < 120,
            pltpu.roll(own, 256 - 120, 1),
            jnp.where(lane < 240, -pltpu.roll(own, 120, 1), 0.0),
        )
        for f in range(GROUP):
            keep = lane % GROUP == f
            both = jnp.concatenate([jnp.where(keep, own, 0.0), jnp.where(keep, turned, 0.0)], axis=0)
            left_ref[64 * f : 64 * f + 64, :] = both.astype(BF16)
        right = all_ref[:, :, lanes].reshape(1024, 256)
        first = 0
        for step in (2, 2, 4, 4) if g == 0 else (4, 4, 4):
            at = len(copies)
            slot = at % SLOTS
            if at >= SLOTS:
                copies[at - SLOTS].wait()
            left = left_ref[64 * first : 64 * (first + step), :]
            prod = lax.dot_general(left, right, (((1,), (1,)), ((), ())), preferred_element_type=F32)
            slot_ref[slot, 0:step] = (prod * (1.0 / WIN)).reshape(step, 2, 32, 1024)
            copy = pltpu.make_async_copy(
                slot_ref.at[slot, pl.ds(0, step)],
                out_ref.at[pl.ds(GROUP * g + first, step)],
                sem.at[slot],
            )
            copy.start()
            copies.append(copy)
            first += step
    for copy in copies[-SLOTS:]:
        copy.wait()


def correlate(own, everyone):
    vmem = pl.BlockSpec(memory_space=pltpu.VMEM)
    return pl.pallas_call(
        correlate_kernel,
        out_shape=jax.ShapeDtypeStruct((60, 2, 32, 1024), F32),
        in_specs=[vmem, vmem],
        out_specs=pl.BlockSpec(memory_space=pltpu.HBM),
        scratch_shapes=[
            pltpu.VMEM((64 * GROUP, 256), BF16),
            pltpu.VMEM((SLOTS, STEP, 2, 32, 1024), F32),
            pltpu.SemaphoreType.DMA((SLOTS,)),
        ],
        compiler_params=pltpu.CompilerParams(vmem_limit_bytes=32 * 1024 * 1024),
        name="correlate",
    )(own, everyone)


def shards(raw_strain, fir_taps, band_bins, live_mask):
    own, everyone = gather(raw_strain, fir_taps, band_bins, live_mask)
    return correlate(own, everyone.reshape(32, 32, WIDE))


def solution(mesh):
    in_specs = (P("chan", "freq", None), P(), P(), P("chan", "freq"))
    out_specs = P("freq", None, "chan", None)
    return jax.shard_map(shards, mesh=mesh, in_specs=in_specs, out_specs=out_specs, check_vma=False)
```

```python
import functools
import math

import jax
import jax.numpy as jnp
from jax import lax
from jax.experimental import pallas as pl
from jax.experimental.pallas import tpu as pltpu
from jax.sharding import PartitionSpec as P

WIN = 10
DECIM = 10
NT = 1500
TAPS = 20
BINS = 240
ROWS = 8
TILE = 128
SPAN = TILE * DECIM
SAMPLES = WIN * NT * DECIM
TILES = -(-SAMPLES // SPAN)
NTP = 12 * TILE
GROUP = 12
PACK = 5 * TILE
WIDE = 5 * 256
F32 = jnp.float32
BF16 = jnp.bfloat16
I32 = jnp.int32
MESH = pl.DeviceIdType.MESH


def iota(shape, axis):
    return lax.broadcasted_iota(I32, shape, axis)


def build_fir(taps_ref, fir_ref):
    row = iota((80, TAPS), 0)
    phase = row % DECIM
    tap = iota((80, TAPS), 1)
    taps = jnp.broadcast_to(taps_ref[...].astype(F32), (80, TAPS))
    near = jnp.sum(jnp.where(tap == 9 - phase, taps, 0.0), axis=1, keepdims=True)
    far = jnp.sum(jnp.where(tap == 19 - phase, taps, 0.0), axis=1, keepdims=True)
    near = jnp.broadcast_to(near, (80, 256))
    far = jnp.broadcast_to(far, (80, 256))
    gap = iota((80, 256), 1) - iota((80, 256), 0) // DECIM
    for step in range(SPAN // 80):
        block = jnp.where(gap == 8 * step, near, jnp.where(gap == 8 * step + 1, far, 0.0))
        fir_ref[80 * step : 80 * step + 80, :] = block.astype(BF16)


def build_table(bins_ref, table_ref):
    bins = bins_ref[...].astype(F32)
    bins = jnp.concatenate([bins, jnp.zeros((1, 16), F32)], axis=1)
    row = iota((40, 256), 0)
    times = jnp.where(row < 8, row, jnp.where(row < 24, 8 * (row - 8), 128 * (row - 24)))
    product = times.astype(F32) * bins
    turns = jnp.floor(product * (1.0 / NT))
    left = product - turns * NT
    left = jnp.where(left < 0, left + NT, left)
    left = jnp.where(left >= NT, left - NT, left)
    angle = left * F32(2.0 * math.pi / NT)
    re = jnp.cos(angle)
    im = -jnp.sin(angle)
    kept = iota((40, 256), 1) < BINS
    re = jnp.where(kept, re, 0.0)
    im = jnp.where(kept, im, 0.0)
    base_re, base_im = [], []
    for b in range(16):
        tr, ti = re[8 + b : 9 + b], im[8 + b : 9 + b]
        base_re.append(re[0:8] * tr - im[0:8] * ti)
        base_im.append(re[0:8] * ti + im[0:8] * tr)
    base_re = jnp.concatenate(base_re, axis=0)
    base_im = jnp.concatenate(base_im, axis=0)
    for a in range(12):
        tr, ti = re[24 + a : 25 + a], im[24 + a : 25 + a]
        block_re = base_re * tr - base_im * ti
        block_im = base_re * ti + base_im * tr
        if a == 11:
            inside = iota((TILE, 256), 0) < NT - 11 * TILE
            block_re = jnp.where(inside, block_re, 0.0)
            block_im = jnp.where(inside, block_im, 0.0)
        table_ref[TILE * a : TILE * a + TILE, 0:256] = block_re.astype(BF16)
        table_ref[TILE * a : TILE * a + TILE, 256:512] = block_im.astype(BF16)


def build_left(x_ref, left_ref):
    def tile(t):
        return x_ref[0, :, SPAN * t : min(SPAN * t + SPAN, SAMPLES)].astype(F32)

    blocks = [(t, None) for t in range(TILES)]
    for w in range(1, WIN):
        t = NT * w // TILE
        blocks.append((t, NT * DECIM * w - SPAN * t))
    blocks.append((None, None))

    def value(block):
        t, first = block
        if t is None:
            return jnp.zeros((ROWS, SPAN), F32)
        part = tile(t)
        if part.shape[1] < SPAN:
            part = jnp.concatenate([part, jnp.zeros((ROWS, SPAN - part.shape[1]), F32)], axis=1)
        if first is not None:
            part = jnp.where(iota((ROWS, SPAN), 1) < first, 0.0, part)
        return part

    for pair in range(len(blocks) // 2):
        both = jnp.concatenate([value(blocks[2 * pair]), value(blocks[2 * pair + 1])], axis=0)
        left_ref[16 * pair : 16 * pair + 16, :] = both.astype(BF16)


def align_windows(res_ref, dec_ref):
    lane = iota((ROWS, TILE), 1)

    def plain(t):
        main = res_ref[8 * t : 8 * t + 8, 0:TILE]
        if t == 0:
            return main
        return main + res_ref[8 * t - 8 : 8 * t, TILE : 2 * TILE]

    def window(w):
        t = NT * w // TILE
        shift = NT * w - TILE * t
        tiles = [plain(t + u) for u in range(1, 13 if shift else 12)]
        if w == 0:
            first = plain(0)
        else:
            at = 8 * (TILES + w - 1)
            first = res_ref[at : at + 8, 0:TILE]
        tiles = [first] + tiles
        if shift:
            rolled = [pltpu.roll(one, TILE - shift, 1) for one in tiles]
            tiles = [
                jnp.where(lane < TILE - shift, rolled[u], rolled[u + 1]) for u in range(12)
            ]
        return jnp.concatenate(tiles, axis=1)

    for pair in range(WIN // 2):
        both = jnp.concatenate([window(2 * pair), window(2 * pair + 1)], axis=0)
        dec_ref[16 * pair : 16 * pair + 16, :] = both.astype(BF16)


def pack(white, send_ref):
    lane = iota((ROWS, 256), 1)
    segment = lane // GROUP
    wrapped = (lane + 256) // GROUP
    turned = []
    for part in range(2):
        for w in range(WIN):
            spot = part * WIN + w
            piece = white[8 * w : 8 * w + 8, 256 * part : 256 * part + 256]
            turned.append(pltpu.roll(piece, GROUP * spot, 1) if spot else piece)
    for group in range(BINS // GROUP):
        halves = []
        for half in range(2):
            lanes = slice(TILE * half, TILE * half + TILE)
            total = jnp.zeros((ROWS, TILE), F32)
            for spot in range(2 * WIN):
                start = GROUP * (spot + group)
                covers = [
                    at
                    for at in (start, start - 256)
                    if at < TILE * half + TILE and at + GROUP > TILE * half
                ]
                for at in covers:
                    ids = segment if at == start else wrapped
                    total = jnp.where(
                        ids[:, lanes] == spot + group, turned[spot][:, lanes], total
                    )
            halves.append(total)
        dest = jnp.concatenate(halves, axis=1)
        if group:
            dest = pltpu.roll(dest, 256 - GROUP * group, 1)
        both = jnp.concatenate([dest[:, 0:TILE], dest[:, TILE:256]], axis=0)
        z, g = group // 5, group % 5
        send_ref[z, :, TILE * g : TILE * g + TILE] = both.astype(BF16)


def spectra(x_ref, loaded, taps_ref, bins_ref, mask_ref, send_ref, fir_ref, table_ref, left_ref, res_ref, dec_ref):
    build_fir(taps_ref, fir_ref)
    loaded.wait()
    build_left(x_ref, left_ref)
    build_table(bins_ref, table_ref)
    res_ref[...] = jnp.dot(left_ref[...], fir_ref[...], preferred_element_type=F32)
    align_windows(res_ref, dec_ref)
    spectrum = jnp.dot(dec_ref[...], table_ref[...], preferred_element_type=F32)
    power = jnp.sum(spectrum * spectrum, axis=1, keepdims=True) / BINS
    channel = iota((80, 8), 0) % ROWS
    live = jnp.broadcast_to(mask_ref[...].astype(F32), (80, 8))
    live = jnp.sum(jnp.where(channel == iota((80, 8), 1), live, 0.0), axis=1, keepdims=True)
    white = spectrum * (lax.rsqrt(power + 1e-06) * live)
    pack(white, send_ref)


def schedule():
    steps = []

    def begin(h):
        for d in (1, -1, 2):
            steps.append(("near", h, d))
        for v in (1, -1, 2):
            steps.append(("far", h, 0, v))

    def go_on(h):
        for d in (1, -1, 2):
            u = d if d == 2 else -d
            steps.append(("near_wait", h, d))
            for v in (1, -1, 2):
                steps.append(("far", h, u, v))

    def finish(h):
        for u in (0, -1, 1, 2):
            steps.append(("far_wait", h, u))
            steps.append(("share", h, u))

    steps.append(("take", 0))
    begin(0)
    steps.append(("take", 1))
    begin(1)
    go_on(0)
    go_on(1)
    finish(0)
    steps.append(("drain", 0))
    finish(1)
    return steps


SCHEDULE = schedule()


def gather_kernel(
    x_ref, taps_ref, bins_ref, mask_ref, own_ref, all_ref,
    x_here, taps_here, bins_here, mask_here, fir_ref, table_ref, left_ref, res_ref, dec_ref, send_ref, raw,
    in_sem, z_send, z_recv, sent_sem, near_recv, far_recv, share_sem,
):
    z = lax.axis_index("freq")
    b = lax.axis_index("chan")
    x, y, c = b // 8, (b // 2) % 4, b % 2

    def index(xx, yy, cc):
        return (xx % 4 * 4 + yy % 4) * 2 + cc

    sibling = index(x, y, 1 - c)
    peers = [((z + d) % 4, b) for d in (1, 2, 3)]
    peers += [(z, index(x + d, y, c)) for d in (1, 2, 3)]
    peers += [(z, index(x, y + d, c)) for d in (1, 2, 3)]
    peers += [(z, sibling)]
    barrier = pltpu.get_barrier_semaphore()
    for peer in peers:
        pl.semaphore_signal(barrier, inc=1, device_id=peer, device_id_type=MESH)

    loaded = pltpu.make_async_copy(x_ref, x_here, in_sem.at[3])
    loaded.start()
    small = []
    for at, (src, dst) in enumerate(((taps_ref, taps_here), (bins_ref, bins_here), (mask_ref, mask_here))):
        copy = pltpu.make_async_copy(src, dst, in_sem.at[at])
        copy.start()
        small.append(copy)
    for copy in small:
        copy.wait()
    spectra(
        x_here, loaded, taps_here, bins_here, mask_here, send_ref,
        fir_ref, table_ref, left_ref, res_ref, dec_ref,
    )
    pl.semaphore_wait(barrier, len(peers))

    crossing, landed = [], {}
    for d in (2, 1, 3):
        to = (z + d) % 4
        copy = pltpu.make_async_remote_copy(
            src_ref=send_ref.at[to], dst_ref=raw.at[z],
            send_sem=z_send.at[d - 1], recv_sem=z_recv.at[d - 1],
            device_id=(to, b), device_id_type=MESH,
        )
        copy.start()
        crossing.append(copy)
        landed[d] = copy
    raw[z] = send_ref[z]

    def push(region, target, sent, landed):
        pltpu.make_async_remote_copy(
            src_ref=region, dst_ref=region, send_sem=sent, recv_sem=landed,
            device_id=(z, target), device_id_type=MESH,
        ).start()

    def wait_for(region, sem):
        pltpu.make_async_copy(region, region, sem).wait()

    xs = {d: lax.rem(x + d % 4, 4) for d in (0, 1, -1, 2)}
    ys = {d: lax.rem(y + d % 4, 4) for d in (0, 1, -1, 2)}
    along_x = {d: (xs[d] * 4 + y) * 2 + c for d in (1, -1, 2)}
    along_y = {d: (x * 4 + ys[d]) * 2 + c for d in (1, -1, 2)}

    def part(half, route):
        return pl.ds(16 * half, 16), pl.ds(PACK * route, PACK)

    def block(half, route, u):
        xx, yy = (xs[u], y) if route == 0 else (x, ys[u])
        return all_ref.at[(xx, yy, c) + part(half, route)]

    def share(half, route, u):
        if route == 0:
            region = all_ref.at[(xs[u], slice(None), c) + part(half, route)]
        else:
            region = all_ref.at[(slice(None), ys[u], c) + part(half, route)]
        push(region, sibling, sent_sem.at[2], share_sem.at[0])

    def near_sem(half, route, d):
        return near_recv.at[6 * half + 3 * route + (1, -1, 2).index(d)]

    def far_sem(half, route, u):
        return far_recv.at[8 * half + 4 * route + u % 4]

    def unite(half):
        rows = slice(16 * half, 16 * half + 16)
        even = raw[2 * half].astype(F32)
        odd = raw[2 * half + 1].astype(F32)
        low = jnp.concatenate([even[0:8], odd[0:8]], axis=0).astype(BF16)
        high = jnp.concatenate([even[8:16], odd[8:16]], axis=0).astype(BF16)
        for at in range(10):
            source = high if at % 2 else low
            piece = source[:, TILE * (at // 2) : TILE * (at // 2) + TILE]
            lanes = slice(TILE * at, TILE * at + TILE)
            own_ref[rows, lanes] = piece
            all_ref[x, y, c, rows, lanes] = piece

    def arrive(source):
        for d in (1, 2, 3):
            @pl.when((z - source + 4) % 4 == d)
            def _():
                landed[d].wait_recv()

    for kind, half, *rest in SCHEDULE:
        if kind == "take":
            arrive(2 * half)
            arrive(2 * half + 1)
            unite(half)
            continue
        if kind == "drain":
            wait_for(all_ref.at[0, pl.ds(0, 3), 0], sent_sem.at[0])
            wait_for(all_ref.at[pl.ds(0, 3), :, 0], sent_sem.at[1])
            for copy in crossing:
                copy.wait_send()
            continue
        for route in (0, 1):
            if kind == "near":
                to = (along_x if route == 0 else along_y)[rest[0]]
                push(block(half, route, 0), to, sent_sem.at[0], near_sem(half, route, rest[0]))
            elif kind == "near_wait":
                wait_for(block(half, route, 0), near_sem(half, route, rest[0]))
            elif kind == "far":
                u, v = rest
                to = (along_y if route == 0 else along_x)[v]
                push(block(half, route, u), to, sent_sem.at[1], far_sem(half, route, u))
            elif kind == "far_wait":
                three = all_ref.at[(pl.ds(0, 3), 0, 0) + part(half, route)]
                wait_for(three, far_sem(half, route, rest[0]))
            else:
                share(half, route, rest[0])
    wait_for(all_ref.at[:, :, 0], share_sem.at[0])
    wait_for(all_ref.at[:, :, 0], sent_sem.at[2])


def gather(raw_strain, fir_taps, band_bins, live_mask):
    vmem = pl.BlockSpec(memory_space=pltpu.VMEM)
    hbm = pl.BlockSpec(memory_space=pltpu.HBM)
    arrays = (raw_strain, fir_taps.reshape(1, TAPS), band_bins.reshape(1, BINS), live_mask)
    arrays = [pltpu.with_memory_space_constraint(one, pltpu.HBM) for one in arrays]
    return pl.pallas_call(
        gather_kernel,
        out_shape=(
            jax.ShapeDtypeStruct((32, WIDE), BF16),
            jax.ShapeDtypeStruct((4, 4, 2, 32, WIDE), BF16),
        ),
        in_specs=[hbm] * 4,
        out_specs=(vmem, vmem),
        scratch_shapes=[
            pltpu.VMEM((1, ROWS, SAMPLES), BF16),
            pltpu.VMEM((1, TAPS), BF16),
            pltpu.VMEM((1, BINS), I32),
            pltpu.VMEM((1, 8), I32),
            pltpu.VMEM((SPAN, 256), BF16),
            pltpu.VMEM((NTP, 512), BF16),
            pltpu.VMEM((1024, SPAN), BF16),
            pltpu.VMEM((1024, 256), F32),
            pltpu.VMEM((80, NTP), BF16),
            pltpu.VMEM((4, 16, PACK), BF16),
            pltpu.VMEM((4, 16, PACK), BF16),
            pltpu.SemaphoreType.DMA((4,)),
            pltpu.SemaphoreType.DMA((3,)),
            pltpu.SemaphoreType.DMA((3,)),
            pltpu.SemaphoreType.DMA((3,)),
            pltpu.SemaphoreType.DMA((12,)),
            pltpu.SemaphoreType.DMA((16,)),
            pltpu.SemaphoreType.DMA((1,)),
        ],
        compiler_params=pltpu.CompilerParams(
            collective_id=0, has_side_effects=True, vmem_limit_bytes=32 * 1024 * 1024
        ),
        name="gather",
    )(*arrays)


SLOTS = 8
STEP = 4


def correlate_kernel(own_ref, all_ref, out_ref, left_ref, slot_ref, sem):
    lane = iota((32, 256), 1)
    copies = []
    for g in range(5):
        lanes = slice(256 * g, 256 * g + 256)
        own = own_ref[:, lanes].astype(F32)
        turned = jnp.where(
            lane < 120,
            pltpu.roll(own, 256 - 120, 1),
            jnp.where(lane < 240, -pltpu.roll(own, 120, 1), 0.0),
        )
        for f in range(GROUP):
            keep = lane % GROUP == f
            both = jnp.concatenate([jnp.where(keep, own, 0.0), jnp.where(keep, turned, 0.0)], axis=0)
            left_ref[64 * f : 64 * f + 64, :] = both.astype(BF16)
        right = all_ref[:, :, lanes].reshape(1024, 256)
        for first in range(0, GROUP, STEP):
            at = len(copies)
            slot = at % SLOTS
            if at >= SLOTS:
                copies[at - SLOTS].wait()
            left = left_ref[64 * first : 64 * (first + STEP), :]
            prod = lax.dot_general(left, right, (((1,), (1,)), ((), ())), preferred_element_type=F32)
            slot_ref[slot] = (prod * (1.0 / WIN)).reshape(STEP, 2, 32, 1024)
            copy = pltpu.make_async_copy(
                slot_ref.at[slot], out_ref.at[pl.ds(GROUP * g + first, STEP)], sem.at[slot]
            )
            copy.start()
            copies.append(copy)
    for copy in copies[-SLOTS:]:
        copy.wait()


def correlate(own, everyone):
    vmem = pl.BlockSpec(memory_space=pltpu.VMEM)
    return pl.pallas_call(
        correlate_kernel,
        out_shape=jax.ShapeDtypeStruct((60, 2, 32, 1024), F32),
        in_specs=[vmem, vmem],
        out_specs=pl.BlockSpec(memory_space=pltpu.HBM),
        scratch_shapes=[
            pltpu.VMEM((64 * GROUP, 256), BF16),
            pltpu.VMEM((SLOTS, STEP, 2, 32, 1024), F32),
            pltpu.SemaphoreType.DMA((SLOTS,)),
        ],
        compiler_params=pltpu.CompilerParams(vmem_limit_bytes=32 * 1024 * 1024),
        name="correlate",
    )(own, everyone)


def shards(raw_strain, fir_taps, band_bins, live_mask):
    own, everyone = gather(raw_strain, fir_taps, band_bins, live_mask)
    return correlate(own, everyone.reshape(32, 32, WIDE))


def solution(mesh):
    in_specs = (P("chan", "freq", None), P(), P(), P("chan", "freq"))
    out_specs = P("freq", None, "chan", None)
    return jax.shard_map(shards, mesh=mesh, in_specs=in_specs, out_specs=out_specs, check_vma=False)
```
